128 devices in a mesh: row: 8 (over y, core), col: 16 (over x, z).
Axes of the slice: x: 4, y: 4, z: 4, core: 2. Of those that a mesh axis runs over, the one named last changes fastest.
Arguments:
- noise: bfloat16 [8192, 4096], P('row', 'col'), may hold values from -6 to 6
- latents: bfloat16 [16384, 4096], P('col', 'row'), may hold values from -12 to 12
Outputs:
- transported: bfloat16 [8192, 4096], P('row', 'col')
- row_potential: float32 [8192], P('row')
- col_potential: float32 [16384], P('col')
The draws below stay inside these ranges and needn't reach their ends.
All inputs are finite; a program needn't handle non-finite values.
Results may differ from the reference program's by a relative error of at most 0.018.
Values may be sent and summed in bfloat16 or wider, within the bound.
No kernel may reach another device: no remote copies, remote signals or barrier semaphores. Data moves between devices by JAX's collectives and lax.ppermute only.
A program may use at most 64 MiB of HBM per device.

```python
import math
import jax
import jax.numpy as jnp
from jax import lax

LATDIM = 4096
COLS_DEV = 1024
ITERS = 3
NOISE = 8192
LATS = 16384
N_COL = 16


def shared_noise(key):
    values = jax.random.normal(jax.random.fold_in(key, 11), (NOISE, LATDIM), jnp.float32)
    return jnp.clip(values, -6.0, 6.0)


def draw_noise(key, part):
    base = shared_noise(key)
    values = base
    return values.astype(jnp.bfloat16)


def draw_latents(key, part):
    key = jax.random.fold_in(key, 5)
    keys = jax.random.split(key, 2)
    scale = jnp.exp(jax.random.uniform(keys[0], (LATS, 1), jnp.float32, math.log(0.4), math.log(1.6)))
    values = jax.random.normal(keys[1], (LATS, LATDIM), jnp.float32) * scale
    return jnp.clip(values, -12.0, 12.0).astype(jnp.bfloat16)


def setup_inputs(seed: int = 0) -> dict:
    key_list = jax.random.split(jax.random.key(seed), 3)
    noise = draw_noise(jax.random.fold_in(key_list[2], 71), 0)
    latents = draw_latents(jax.random.fold_in(key_list[2], 71), 0)
    return {"noise": noise, "latents": latents}


epsilon = 0.01


def logsum(scores, axis):
    high = jnp.max(scores, axis=axis, keepdims=True)
    total = jnp.sum(jnp.exp(scores - high), axis=axis)
    return jnp.squeeze(high, axis) + jnp.log(total)


def reference(noise, latents):
    cross = jnp.dot(noise, latents.T, preferred_element_type=jnp.float32)
    logits = cross * (2.0 / (LATDIM * epsilon))
    col_potential = jnp.zeros((LATS,), jnp.float32)
    row_potential = jnp.zeros((NOISE,), jnp.float32)
    for step in range(ITERS):
        row_potential = -math.log(NOISE) - logsum(logits + col_potential[None, :], 1)
        col_potential = -math.log(LATS) - logsum(logits + row_potential[:, None], 0)
    plan = jnp.exp(logits + row_potential[:, None] + col_potential[None, :]).astype(jnp.bfloat16)
    plan_blocks = jnp.transpose(plan.reshape(NOISE, N_COL, COLS_DEV), (1, 0, 2))
    lat_blocks = latents.reshape(N_COL, COLS_DEV, LATDIM)

    def add_block(total, pair):
        partial_value = jnp.dot(pair[0], pair[1], preferred_element_type=jnp.float32).astype(jnp.bfloat16)
        return total + partial_value.astype(jnp.float32), None

    numerator, unused = lax.scan(add_block, jnp.zeros((NOISE, LATDIM), jnp.float32), (plan_blocks, lat_blocks))
    mass = jnp.sum(plan.astype(jnp.float32), axis=1)
    transported = (numerator / mass[:, None]).astype(jnp.bfloat16)
    return transported, row_potential, col_potential
```

```python
import functools
import math

import jax
import jax.numpy as jnp
from jax import lax
from jax.experimental import pallas as pl
from jax.experimental.pallas import tpu as pltpu
from jax.sharding import PartitionSpec as P

ITERS = 3
EPSILON = 0.01
LOG2E = math.log2(math.e)
LN2 = math.log(2.0)
NX, NY, NZ, NC = 4, 4, 4, 2

F32 = jnp.float32
BF16 = jnp.bfloat16


def shift_z(by):
    return [(x * NZ + z, x * NZ + (z + by) % NZ) for x in range(NX) for z in range(NZ)]


def shift_x(by):
    return [(x * NZ + z, (x + by) % NX * NZ + z) for x in range(NX) for z in range(NZ)]


def shift_y(by):
    return [(y * NC + c, (y + by) % NY * NC + c) for y in range(NY) for c in range(NC)]


def swap_core():
    return [(y * NC + c, y * NC + 1 - c) for y in range(NY) for c in range(NC)]


def logadd(parts):
    high = functools.reduce(jnp.maximum, parts)
    total = functools.reduce(jnp.add, [jnp.exp2(p - high) for p in parts])
    return high + jnp.log2(total)


def over(value, axis, perms, combine):
    return combine([value] + [lax.ppermute(value, axis, p) for p in perms])


def over_col(value, combine):
    value = over(value, "col", [shift_z(b) for b in (1, 3, 2)], combine)
    return over(value, "col", [shift_x(b) for b in (1, 3, 2)], combine)


def over_row(value, combine):
    value = over(value, "row", [swap_core()], combine)
    return over(value, "row", [shift_y(b) for b in (1, 3, 2)], combine)


def eye():
    return lax.broadcasted_iota(jnp.int32, (128, 128), 0) == lax.broadcasted_iota(
        jnp.int32, (128, 128), 1
    )


def to_lanes(column):
    mask = eye()
    return jnp.concatenate(
        [
            jnp.sum(jnp.where(mask, column[at : at + 128], 0.0), axis=0, keepdims=True)
            for at in range(0, column.shape[0], 128)
        ],
        axis=1,
    )


def to_sublanes(line):
    mask = eye()
    return jnp.concatenate(
        [
            jnp.sum(jnp.where(mask, line[:, at : at + 128], 0.0), axis=1, keepdims=True)
            for at in range(0, line.shape[1], 128)
        ],
        axis=0,
    )


def row_lse_block(read, rows, out):
    step = 32
    columns = []
    for at in range(0, rows, step):
        t = read(at, step)
        high = jnp.max(t, axis=1, keepdims=True)
        total = jnp.sum(jnp.exp2(t - high), axis=1, keepdims=True)
        columns.append(high + jnp.log2(total))
    out[...] = to_lanes(jnp.concatenate(columns, axis=0))


def cross_kernel(scale, noise_ref, lat_ref, logits_ref, lse_ref):
    cross = lax.dot_general(
        noise_ref[...], lat_ref[...], (((1,), (1,)), ((), ())), preferred_element_type=F32
    )
    logits_ref[...] = cross * scale
    row_lse_block(lambda at, n: logits_ref[pl.ds(at, n), :], noise_ref.shape[0], lse_ref)


def cross_call(noise, lat, scale):
    rows, width = noise.shape
    cols = lat.shape[0]
    block = 256
    return pl.pallas_call(
        functools.partial(cross_kernel, scale),
        grid=(rows // block,),
        in_specs=[
            pl.BlockSpec((block, width), lambda i: (i, 0)),
            pl.BlockSpec((cols, width), lambda i: (0, 0)),
        ],
        out_specs=[
            pl.BlockSpec((block, cols), lambda i: (i, 0)),
            pl.BlockSpec((1, block), lambda i: (0, i)),
        ],
        out_shape=[
            jax.ShapeDtypeStruct((rows, cols), F32),
            jax.ShapeDtypeStruct((1, rows), F32),
        ],
        compiler_params=pltpu.CompilerParams(vmem_limit_bytes=40 * 2**20),
        name="cross",
    )(noise, lat)


def row_kernel(logits_ref, colpot_ref, lse_ref):
    colpot = colpot_ref[...]
    row_lse_block(
        lambda at, n: logits_ref[pl.ds(at, n), :] + colpot, logits_ref.shape[0], lse_ref
    )


def row_call(logits, colpot):
    rows, cols = logits.shape
    block = 256
    return pl.pallas_call(
        row_kernel,
        grid=(rows // block,),
        in_specs=[
            pl.BlockSpec((block, cols), lambda i: (i, 0)),
            pl.BlockSpec((1, cols), lambda i: (0, 0)),
        ],
        out_specs=pl.BlockSpec((1, block), lambda i: (0, i)),
        out_shape=jax.ShapeDtypeStruct((1, rows), F32),
        compiler_params=pltpu.CompilerParams(vmem_limit_bytes=16 * 2**20),
        name="row_lse",
    )(logits, colpot)


def col_kernel(logits_ref, rowpot_ref, lse_ref, part_ref):
    step = pl.program_id(0)
    rows, cols = logits_ref.shape
    rowpot = jnp.broadcast_to(to_sublanes(rowpot_ref[...]), (rows, 128))
    lines = []
    for at in range(0, cols, 128):
        t = logits_ref[:, pl.ds(at, 128)] + rowpot
        high = jnp.max(t, axis=0, keepdims=True)
        total = jnp.sum(jnp.exp2(t - high), axis=0, keepdims=True)
        lines.append(high + jnp.log2(total))
    part_ref[pl.ds(step, 1), :] = jnp.concatenate(lines, axis=1)

    @pl.when(step == pl.num_programs(0) - 1)
    def finish():
        parts = part_ref[...]
        high = jnp.max(parts, axis=0, keepdims=True)
        total = jnp.sum(jnp.exp2(parts - high), axis=0, keepdims=True)
        lse_ref[...] = high + jnp.log2(total)


def col_call(logits, rowpot):
    rows, cols = logits.shape
    block = 256
    return pl.pallas_call(
        col_kernel,
        grid=(rows // block,),
        in_specs=[
            pl.BlockSpec((block, cols), lambda i: (i, 0)),
            pl.BlockSpec((1, block), lambda i: (0, i)),
        ],
        out_specs=pl.BlockSpec((1, cols), lambda i: (0, 0)),
        out_shape=jax.ShapeDtypeStruct((1, cols), F32),
        scratch_shapes=[pltpu.VMEM((rows // block, cols), F32)],
        compiler_params=pltpu.CompilerParams(vmem_limit_bytes=16 * 2**20),
        name="col_lse",
    )(logits, rowpot)


def plan_kernel(logits_ref, rowpot_ref, colpot_ref, lat_ref, share_ref, mass_ref):
    rowpot = to_sublanes(rowpot_ref[...])
    plan = jnp.exp2(logits_ref[...] + rowpot + colpot_ref[...]).astype(BF16)
    mass_ref[...] = to_lanes(jnp.sum(plan.astype(F32), axis=1, keepdims=True))
    share_ref[...] = jnp.dot(plan, lat_ref[...], preferred_element_type=F32).astype(BF16)


def plan_call(logits, rowpot, colpot, lat):
    rows, cols = logits.shape
    width = lat.shape[1]
    block = 256
    return pl.pallas_call(
        plan_kernel,
        grid=(rows // block,),
        in_specs=[
            pl.BlockSpec((block, cols), lambda i: (i, 0)),
            pl.BlockSpec((1, block), lambda i: (0, i)),
            pl.BlockSpec((1, cols), lambda i: (0, 0)),
            pl.BlockSpec((cols, width), lambda i: (0, 0)),
        ],
        out_specs=[
            pl.BlockSpec((block, width), lambda i: (i, 0)),
            pl.BlockSpec((1, block), lambda i: (0, i)),
        ],
        out_shape=[
            jax.ShapeDtypeStruct((rows, width), BF16),
            jax.ShapeDtypeStruct((1, rows), F32),
        ],
        compiler_params=pltpu.CompilerParams(vmem_limit_bytes=48 * 2**20),
        name="plan",
    )(logits, rowpot, colpot, lat)


def on_device(noise, latents):
    whole_lat = lax.all_gather(latents, "row", axis=1, tiled=True)
    whole_noise = lax.all_gather(noise, "col", axis=1, tiled=True)
    width = whole_lat.shape[1]
    noise_count = noise.shape[0] * lax.axis_size("row")
    latent_count = latents.shape[0] * lax.axis_size("col")
    logits, lse = cross_call(whole_noise, whole_lat, 2.0 / (width * EPSILON) * LOG2E)
    for step in range(ITERS):
        if step:
            lse = row_call(logits, colpot)
        rowpot = -math.log2(noise_count) - over_col(lse, logadd)
        colpot = -math.log2(latent_count) - over_row(col_call(logits, rowpot), logadd)
    share, mass = plan_call(logits, rowpot, colpot, whole_lat)
    mass = over_col(mass, lambda parts: functools.reduce(jnp.add, parts))
    total = lax.psum_scatter(share, "col", scatter_dimension=1, tiled=True).astype(F32)
    transported = (total / mass.reshape(-1, 1)).astype(BF16)
    return (transported, rowpot.reshape(-1) * LN2, colpot.reshape(-1) * LN2)


def solution(mesh):
    in_specs = (P("row", "col"), P("col", "row"))
    out_specs = (P("row", "col"), P("row"), P("col"))
    return jax.shard_map(
        on_device, mesh=mesh, in_specs=in_specs, out_specs=out_specs, check_vma=False
    )
```

```python
import functools
import math

import jax
import jax.numpy as jnp
from jax import lax
from jax.experimental import pallas as pl
from jax.experimental.pallas import tpu as pltpu
from jax.sharding import PartitionSpec as P

ITERS = 3
EPSILON = 0.01
LOG2E = math.log2(math.e)
LN2 = math.log(2.0)
NX, NY, NZ, NC = 4, 4, 4, 2

F32 = jnp.float32
BF16 = jnp.bfloat16


def shift_z(by):
    return [(x * NZ + z, x * NZ + (z + by) % NZ) for x in range(NX) for z in range(NZ)]


def shift_x(by):
    return [(x * NZ + z, (x + by) % NX * NZ + z) for x in range(NX) for z in range(NZ)]


def shift_y(by):
    return [(y * NC + c, (y + by) % NY * NC + c) for y in range(NY) for c in range(NC)]


def swap_core():
    return [(y * NC + c, y * NC + 1 - c) for y in range(NY) for c in range(NC)]


def logadd(parts):
    high = functools.reduce(jnp.maximum, parts)
    total = functools.reduce(jnp.add, [jnp.exp2(p - high) for p in parts])
    return high + jnp.log2(total)


def over(value, axis, perms, combine):
    return combine([value] + [lax.ppermute(value, axis, p) for p in perms])


def over_col(value, combine):
    value = over(value, "col", [shift_z(b) for b in (1, 3, 2)], combine)
    return over(value, "col", [shift_x(b) for b in (1, 3, 2)], combine)


def over_row(value, combine):
    value = over(value, "row", [swap_core()], combine)
    return over(value, "row", [shift_y(b) for b in (1, 3, 2)], combine)


BOTH = ("row", "col")


def shift_noise(by, first):
    pairs = []
    for y in range(NY):
        for c in range(NC):
            for x in range(NX):
                for z in range(NZ):
                    to_x, to_z = (x, (z + by) % NZ) if (c == 0) == first else ((x + by) % NX, z)
                    base = (y * NC + c) * NX * NZ
                    pairs.append((base + x * NZ + z, base + to_x * NZ + to_z))
    return pairs


def spread_y():
    return [
        (y * NC + c, (y + 1 - 2 * c) % NY * NC + c) for y in range(NY) for c in range(NC)
    ]


ORDER = (0, 3, 1, 2)


def hop_f(value, by):
    return lax.ppermute(value, BOTH, shift_noise(by, True))


def hop_s(value, by):
    return lax.ppermute(value, BOTH, shift_noise(by, False))


def block_at(df, ds):
    core = lax.axis_index("row") % NC
    col = lax.axis_index("col")
    dz = jnp.where(core == 0, df, ds)
    dx = jnp.where(core == 0, ds, df)
    return (col // NZ + dx) % NX * NZ + (col % NZ + dz) % NZ


def gather_noise(noise):
    rows = noise.shape[0]
    half = rows // 2
    line = [noise, hop_f(noise, 1), hop_f(noise, -1), hop_f(noise, 2)]
    top = jnp.concatenate([v[:half] for v in line], axis=0)
    end = jnp.concatenate([v[half:] for v in line], axis=0)
    top_m, end_p = hop_s(top, 1), hop_s(end, -1)
    end_m, top_p = hop_s(end, 1), hop_s(top, -1)
    top_far, end_far = hop_s(top_m, 1), hop_s(end_p, -1)
    pieces, plan, at = [], [], []
    for v, df in zip(line, ORDER):
        plan.append((len(pieces), 0, rows, 0, len(at)))
        at.append(block_at(df, 0))
        pieces.append(v)
    for v, row, ds in (
        (top_m, 0, 3), (end_m, half, 3), (top_p, 0, 1), (end_p, half, 1),
        (top_far, 0, 2), (end_far, half, 2),
    ):
        for k, df in enumerate(ORDER):
            plan.append((len(pieces), k * half, half, row, len(at)))
            at.append(block_at(df, ds))
        pieces.append(v)
    return pieces, plan, at


def gather_latents(latents):
    cols = latents.shape[0]
    swap = lambda v: lax.ppermute(v, "row", swap_core())
    onward = lambda v: lax.ppermute(v, "row", spread_y())
    near = onward(latents)
    other = swap(latents)
    near_2 = onward(other)
    far = onward(near)
    pieces = [latents, other, near, near_2, far, swap(near), swap(near_2), swap(far)]
    row = lax.axis_index("row")
    y, core = row // NC, row % NC
    block = lambda dy, flip: (y + dy) % NY * NC + (core if not flip else 1 - core)
    back = jnp.where(core == 0, 3, 1)
    plan = [(k, 0, cols, 0, k) for k in range(8)]
    at = [
        block(0, False), block(0, True),
        block(back, False), block(back, True), block(2, False),
        block(4 - back, True), block(4 - back, False), block(2, True),
    ]
    return pieces, plan, at


def scatter_sum(plan, lat, far_top, far_end):
    blocks = lambda ds: jnp.stack([block_at(df, ds) for df in ORDER]).astype(jnp.int32)
    after, before = blocks(1), blocks(3)
    far_top, far_end = hop_s(far_top, 1), hop_s(far_end, -1)
    end_m = hop_s(share_call(plan, lat, after, 1), 1)
    top_p = hop_s(share_call(plan, lat, before, 0), -1)
    own = share_call(plan, lat, blocks(0), None)
    top_m = hop_s(share_call(plan, lat, after, 0, far_top), 1)
    end_p = hop_s(share_call(plan, lat, before, 1, far_end), -1)
    half, width = top_m.shape[0], top_m.shape[1] // 4
    sums = []
    for k in range(4):
        lanes = slice(k * width, (k + 1) * width)
        top = own[:half, lanes] + top_m[:, lanes].astype(F32) + top_p[:, lanes].astype(F32)
        end = own[half:, lanes] + end_m[:, lanes].astype(F32) + end_p[:, lanes].astype(F32)
        sums.append(jnp.concatenate([top, end], axis=0))
    total = sums[0]
    for value, df in zip(sums[1:], ORDER[1:]):
        total = total + hop_f(value.astype(BF16), df).astype(F32)
    return total


def eye():
    return lax.broadcasted_iota(jnp.int32, (128, 128), 0) == lax.broadcasted_iota(
        jnp.int32, (128, 128), 1
    )


def to_lanes(column):
    mask = eye()
    return jnp.concatenate(
        [
            jnp.sum(jnp.where(mask, column[at : at + 128], 0.0), axis=0, keepdims=True)
            for at in range(0, column.shape[0], 128)
        ],
        axis=1,
    )


def to_sublanes(line):
    mask = eye()
    return jnp.concatenate(
        [
            jnp.sum(jnp.where(mask, line[:, at : at + 128], 0.0), axis=1, keepdims=True)
            for at in range(0, line.shape[1], 128)
        ],
        axis=0,
    )


def row_lse_block(read, rows, out):
    step = 32
    columns = []
    for at in range(0, rows, step):
        t = read(at, step)
        high = jnp.max(t, axis=1, keepdims=True)
        total = jnp.sum(jnp.exp2(t - high), axis=1, keepdims=True)
        columns.append(high + jnp.log2(total))
    out[...] = to_lanes(jnp.concatenate(columns, axis=0))


def cross_kernel(scale, noise_plan, lat_plan, at_ref, *refs):
    counts = (1 + max(p[0] for p in noise_plan), 1 + max(p[0] for p in lat_plan))
    noise_refs, lat_refs = refs[: counts[0]], refs[counts[0] : sum(counts)]
    logits_ref, lse_ref, lat_out, noise_buf, lat_buf, noise_sem, lat_sem, out_sem = refs[sum(counts) :]
    rows, width = noise_buf.shape
    part = width // 4
    quarters = [lax.rem(at_ref[at_ref.shape[0] - 1] + k, 4) for k in (0, 3, 1, 2)]
    for quarter in quarters:
        for plan, sources, buf, sem in (
            (lat_plan, lat_refs, lat_buf, lat_sem),
            (noise_plan, noise_refs, noise_buf, noise_sem),
        ):
            for piece, first, count, row, entry in plan:
                wide = sources[piece].shape[1]
                lane = at_ref[entry] * wide

                @pl.when(lax.div(lane, part) == quarter)
                def start():
                    pltpu.make_async_copy(
                        sources[piece].at[pl.ds(first, count), :],
                        buf.at[pl.ds(row, count), pl.ds(pl.multiple_of(lane, wide), wide)],
                        sem.at[quarter],
                    ).start()

    block = 256
    outs = []
    for j, quarter in enumerate(quarters):
        lanes = pl.ds(pl.multiple_of(quarter * part, part), part)
        for buf, sem in ((lat_buf, lat_sem), (noise_buf, noise_sem)):
            pltpu.make_async_copy(buf.at[:, lanes], buf.at[:, lanes], sem.at[quarter]).wait()
        outs.append(pltpu.make_async_copy(lat_buf.at[:, lanes], lat_out.at[:, lanes], out_sem.at[j]))
        outs[-1].start()

        def some_rows(i, _):
            at = pl.ds(pl.multiple_of(i * block, block), block)
            cross = lax.dot_general(
                noise_buf[at, lanes],
                lat_buf[:, lanes],
                (((1,), (1,)), ((), ())),
                preferred_element_type=F32,
            )
            if j:
                cross = logits_ref[at, :] + cross
            if j == 3:
                cross = cross * scale
            logits_ref[at, :] = cross
            if j == 3:
                row_lse_block(
                    lambda k, n: logits_ref[pl.ds(pl.multiple_of(i * block, block) + k, n), :],
                    block,
                    lse_ref.at[:, at],
                )
            return 0

        lax.fori_loop(0, rows // block, some_rows, 0)
    for out in outs:
        out.wait()


def cross_call(noise, lat, cols, width, scale):
    pieces = noise[0] + lat[0]
    rows = noise[0][0].shape[0]
    shift = len(noise[2])
    lat_plan = [(p, f, c, r, e + shift) for p, f, c, r, e in lat[1]]
    first = lax.axis_index("col") // NZ
    return pl.pallas_call(
        functools.partial(cross_kernel, scale, noise[1], lat_plan),
        in_specs=[pl.BlockSpec(memory_space=pltpu.SMEM)]
        + [pl.BlockSpec(memory_space=pltpu.HBM)] * len(pieces),
        out_specs=[
            pl.BlockSpec(memory_space=pltpu.VMEM),
            pl.BlockSpec(memory_space=pltpu.VMEM),
            pl.BlockSpec(memory_space=pltpu.HBM),
        ],
        out_shape=[
            jax.ShapeDtypeStruct((rows, cols), F32),
            jax.ShapeDtypeStruct((1, rows), F32),
            jax.ShapeDtypeStruct((cols, width), BF16),
        ],
        scratch_shapes=[
            pltpu.VMEM((rows, width), BF16),
            pltpu.VMEM((cols, width), BF16),
            pltpu.SemaphoreType.DMA((4,)),
            pltpu.SemaphoreType.DMA((4,)),
            pltpu.SemaphoreType.DMA((4,)),
        ],
        cost_estimate=pl.CostEstimate(
            flops=2 * rows * cols * width,
            bytes_accessed=2 * (rows + 2 * cols) * width + 4 * rows * cols,
            transcendentals=rows * cols,
        ),
        compiler_params=pltpu.CompilerParams(vmem_limit_bytes=32 * 2**20),
        name="cross",
    )(jnp.stack(noise[2] + lat[2] + [first]).astype(jnp.int32), *pieces)


def row_kernel(logits_ref, colpot_ref, lse_ref):
    colpot = colpot_ref[...]
    row_lse_block(
        lambda at, n: logits_ref[pl.ds(at, n), :] + colpot, logits_ref.shape[0], lse_ref
    )


def row_call(logits, colpot):
    rows, cols = logits.shape
    block = 256
    return pl.pallas_call(
        row_kernel,
        grid=(rows // block,),
        in_specs=[
            pl.BlockSpec((block, cols), lambda i: (i, 0)),
            pl.BlockSpec((1, cols), lambda i: (0, 0)),
        ],
        out_specs=pl.BlockSpec((1, block), lambda i: (0, i)),
        out_shape=jax.ShapeDtypeStruct((1, rows), F32),
        compiler_params=pltpu.CompilerParams(vmem_limit_bytes=16 * 2**20),
        name="row_lse",
    )(logits, colpot)


def col_kernel(logits_ref, rowpot_ref, lse_ref, part_ref):
    step = pl.program_id(0)
    rows, cols = logits_ref.shape
    rowpot = jnp.broadcast_to(to_sublanes(rowpot_ref[...]), (rows, 128))
    lines = []
    for at in range(0, cols, 128):
        t = logits_ref[:, pl.ds(at, 128)] + rowpot
        high = jnp.max(t, axis=0, keepdims=True)
        total = jnp.sum(jnp.exp2(t - high), axis=0, keepdims=True)
        lines.append(high + jnp.log2(total))
    part_ref[pl.ds(step, 1), :] = jnp.concatenate(lines, axis=1)

    @pl.when(step == pl.num_programs(0) - 1)
    def finish():
        parts = part_ref[...]
        high = jnp.max(parts, axis=0, keepdims=True)
        total = jnp.sum(jnp.exp2(parts - high), axis=0, keepdims=True)
        lse_ref[...] = high + jnp.log2(total)


def col_call(logits, rowpot):
    rows, cols = logits.shape
    block = 256
    return pl.pallas_call(
        col_kernel,
        grid=(rows // block,),
        in_specs=[
            pl.BlockSpec((block, cols), lambda i: (i, 0)),
            pl.BlockSpec((1, block), lambda i: (0, i)),
        ],
        out_specs=pl.BlockSpec((1, cols), lambda i: (0, 0)),
        out_shape=jax.ShapeDtypeStruct((1, cols), F32),
        scratch_shapes=[pltpu.VMEM((rows // block, cols), F32)],
        compiler_params=pltpu.CompilerParams(vmem_limit_bytes=16 * 2**20),
        name="col_lse",
    )(logits, rowpot)


def plan_kernel(blocks_ref, logits_ref, rowpot_ref, colpot_ref, lat_ref, plan_ref, mass_ref, top_ref, end_ref):
    rows = logits_ref.shape[0]
    half = rows // 2

    @pl.when(pl.program_id(0) == 0)
    def make_plan():
        colpot = colpot_ref[...]
        step = 128
        for at in range(0, rows, step):
            rowpot = to_sublanes(rowpot_ref[:, pl.ds(at, step)])
            plan = jnp.exp2(logits_ref[pl.ds(at, step), :] + rowpot + colpot).astype(BF16)
            plan_ref[pl.ds(at, step), :] = plan
            mass = jnp.sum(plan.astype(F32), axis=1, keepdims=True)
            mass_ref[:, pl.ds(at, step)] = to_lanes(mass)

    lat = lat_ref[...]
    top_ref[...] = jnp.dot(plan_ref[:half, :], lat, preferred_element_type=F32).astype(BF16)
    end_ref[...] = jnp.dot(plan_ref[half:, :], lat, preferred_element_type=F32).astype(BF16)


def plan_call(logits, rowpot, colpot, lat, blocks):
    rows, cols = logits.shape
    width = lat.shape[1] // (NX * NZ)
    whole = lambda i, b: (0, 0)
    return pl.pallas_call(
        plan_kernel,
        grid_spec=pltpu.PrefetchScalarGridSpec(
            num_scalar_prefetch=1,
            grid=(4,),
            in_specs=[
                pl.BlockSpec((rows, cols), whole),
                pl.BlockSpec((1, rows), whole),
                pl.BlockSpec((1, cols), whole),
                pl.BlockSpec((cols, width), lambda i, b: (0, b[i])),
            ],
            out_specs=[
                pl.BlockSpec((rows, cols), whole),
                pl.BlockSpec((1, rows), whole),
                pl.BlockSpec((rows // 2, width), lambda i, b: (0, i)),
                pl.BlockSpec((rows // 2, width), lambda i, b: (0, i)),
            ],
        ),
        out_shape=[
            jax.ShapeDtypeStruct((rows, cols), BF16),
            jax.ShapeDtypeStruct((1, rows), F32),
            jax.ShapeDtypeStruct((rows // 2, 4 * width), BF16),
            jax.ShapeDtypeStruct((rows // 2, 4 * width), BF16),
        ],
        cost_estimate=pl.CostEstimate(
            flops=2 * rows * cols * 4 * width,
            bytes_accessed=2 * (rows + cols) * 4 * width + 6 * rows * cols,
            transcendentals=rows * cols,
        ),
        compiler_params=pltpu.CompilerParams(vmem_limit_bytes=32 * 2**20),
        name="plan",
    )(blocks, logits, rowpot, colpot, lat)


def share_kernel(blocks_ref, plan_ref, lat_ref, *refs):
    share = jnp.dot(plan_ref[...], lat_ref[...], preferred_element_type=F32)
    if len(refs) == 2:
        share = share + refs[0][...].astype(F32)
    refs[-1][...] = share.astype(refs[-1].dtype)


def share_call(plan, lat, blocks, part, more=None):
    rows, cols = plan.shape
    width = lat.shape[1] // (NX * NZ)
    count, first = (rows, 0) if part is None else (rows // 2, part)
    spot = pl.BlockSpec((count, width), lambda i, b: (0, i))
    return pl.pallas_call(
        share_kernel,
        grid_spec=pltpu.PrefetchScalarGridSpec(
            num_scalar_prefetch=1,
            grid=(4,),
            in_specs=[
                pl.BlockSpec((count, cols), lambda i, b: (first, 0)),
                pl.BlockSpec((cols, width), lambda i, b: (0, b[i])),
            ]
            + ([] if more is None else [spot]),
            out_specs=spot,
        ),
        out_shape=jax.ShapeDtypeStruct((count, 4 * width), F32 if part is None else BF16),
        cost_estimate=pl.CostEstimate(
            flops=2 * count * cols * 4 * width,
            bytes_accessed=2 * (count * cols + cols * 4 * width + 2 * count * 4 * width),
            transcendentals=0,
        ),
        compiler_params=pltpu.CompilerParams(vmem_limit_bytes=24 * 2**20),
        name="share",
    )(blocks, plan, lat, *([] if more is None else [more]))


def on_device(noise, latents):
    width = latents.shape[1] * lax.axis_size("row")
    noise_count = noise.shape[0] * lax.axis_size("row")
    latent_count = latents.shape[0] * lax.axis_size("col")
    logits, lse, whole_lat = cross_call(
        gather_noise(noise),
        gather_latents(latents),
        latents.shape[0],
        width,
        2.0 / (width * EPSILON) * LOG2E,
    )
    for step in range(ITERS):
        if step:
            lse = row_call(logits, colpot)
        rowpot = -math.log2(noise_count) - over_col(lse, logadd)
        colpot = -math.log2(latent_count) - over_row(col_call(logits, rowpot), logadd)
    far = jnp.stack([block_at(df, 2) for df in ORDER]).astype(jnp.int32)
    plan, mass, far_top, far_end = plan_call(logits, rowpot, colpot, whole_lat, far)
    total = scatter_sum(plan, whole_lat, far_top, far_end)
    mass = over_col(mass, lambda parts: functools.reduce(jnp.add, parts))
    transported = (total / mass.reshape(-1, 1)).astype(BF16)
    return (transported, rowpot.reshape(-1) * LN2, colpot.reshape(-1) * LN2)


def solution(mesh):
    in_specs = (P("row", "col"), P("col", "row"))
    out_specs = (P("row", "col"), P("row"), P("col"))
    return jax.shard_map(
        on_device, mesh=mesh, in_specs=in_specs, out_specs=out_specs, check_vma=False
    )
```

```python
import functools
import math

import jax
import jax.numpy as jnp
from jax import lax
from jax.experimental import pallas as pl
from jax.experimental.pallas import tpu as pltpu
from jax.sharding import PartitionSpec as P

ITERS = 3
EPSILON = 0.01
LOG2E = math.log2(math.e)
LN2 = math.log(2.0)
NX, NY, NZ, NC = 4, 4, 4, 2

F32 = jnp.float32
BF16 = jnp.bfloat16


def shift_z(by):
    return [(x * NZ + z, x * NZ + (z + by) % NZ) for x in range(NX) for z in range(NZ)]


def shift_x(by):
    return [(x * NZ + z, (x + by) % NX * NZ + z) for x in range(NX) for z in range(NZ)]


def shift_y(by):
    return [(y * NC + c, (y + by) % NY * NC + c) for y in range(NY) for c in range(NC)]


def swap_core():
    return [(y * NC + c, y * NC + 1 - c) for y in range(NY) for c in range(NC)]


def logadd(parts):
    high = functools.reduce(jnp.maximum, parts)
    total = functools.reduce(jnp.add, [jnp.exp2(p - high) for p in parts])
    return high + jnp.log2(total)


BOTH = ("row", "col")


def spread_y():
    return [
        (y * NC + c, (y + 1 - 2 * c) % NY * NC + c) for y in range(NY) for c in range(NC)
    ]


def everywhere(perms):
    count = NX * NZ
    return [
        (row * count + a, row * count + b) for row in range(NY * NC) for a, b in perms[row % NC]
    ]


def around(value, axis, spread, opposite, combine):
    far = lax.ppermute(value, axis, opposite)
    near = lax.ppermute(value, axis, spread)
    return combine([value, far, near, lax.ppermute(near, "row", swap_core())])


def over_col(value, combine):
    mine = lax.axis_index("row") % NC == 0
    other = lax.ppermute(value, "row", swap_core())
    both = jnp.concatenate(
        [jnp.where(mine, value, other), jnp.where(mine, other, value)], axis=0
    )
    for shift in (shift_z, shift_x):
        both = around(both, BOTH, everywhere([shift(1), shift(-1)]), everywhere([shift(2)] * 2), combine)
    return jnp.where(mine, both[:1], both[1:])


def over_row(value, combine):
    value = combine([value, lax.ppermute(value, "row", swap_core())])
    return around(value, "row", spread_y(), shift_y(2), combine)


ORDER = (0, 1, 3, 2)


def hop_f(value, by):
    return lax.ppermute(value, BOTH, everywhere([shift_z(by), shift_x(by)]))


def hop_s(value, by):
    return lax.ppermute(value, BOTH, everywhere([shift_x(by), shift_z(by)]))


def gather(noise, latents):
    rows, width = noise.shape
    half = rows // 2
    swap = lambda v: lax.ppermute(v, "row", swap_core())
    opposite = hop_f(noise, 2)
    line = [noise, hop_f(noise, -1), hop_f(noise, 1), opposite]
    near = lax.ppermute(latents, "row", spread_y())
    away = lax.ppermute(latents, "row", [(b, a) for a, b in spread_y()])
    top = jnp.concatenate([v[:half] for v in line], axis=0)
    end = jnp.concatenate([v[half:] for v in line], axis=0)
    after, _, _ = lax.optimization_barrier((near, top, end))
    top_m, end_p = hop_s(top, 1), hop_s(end, -1)
    end_m, top_p = hop_s(end, 1), hop_s(top, -1)
    far = lax.ppermute(after, "row", spread_y())
    top_far, end_far = hop_s(top_m, 1), hop_s(end_p, -1)
    split = lambda v: v.reshape(4, half, width)
    lat = [latents, swap(latents), near, swap(near), away, swap(away), far, swap(far)]
    return (
        line,
        [split(v) for v in (top_p, end_p, top_m, end_m)],
        [split(top_far), split(end_far)],
        lat,
    )


def latent_spots():
    row, col = lax.axis_index("row"), lax.axis_index("col")
    y, core = row // NC, row % NC
    block = lambda dy, flip: (y + dy) % NY * NC + (core if not flip else 1 - core)
    back = jnp.where(core == 0, 3, 1)
    rows = [
        block(0, False), block(0, True), block(back, False), block(4 - back, True),
        block(4 - back, False), block(back, True), block(2, False), block(2, True),
    ]
    at = (jnp.stack(rows)[:, None] * 2 + jnp.arange(2)[None, :]).reshape(-1)
    dx, dz = (at // NZ - col // NZ) % NX, (at % NZ - col % NZ) % NZ
    df, ds = jnp.where(core == 0, dz, dx), jnp.where(core == 0, dx, dz)
    rank = lambda d: jnp.where(d < 2, d, 5 - d)
    return (rank(ds) * 4 + rank(df)).astype(jnp.int32)


def scatter_sum(plan, spots, lat, far_top, far_end, mass, rowpot, colpot):
    barrier = lax.optimization_barrier
    far_top, far_end = hop_s(far_top, 1), hop_s(far_end, -1)
    end, top, after, before = share_call(spots, lat, plan, mass)
    end_m, top_p = hop_s(end, 1), hop_s(top, -1)
    top, end = onward_call(plan, after, before, mass, far_top, far_end)
    top_m, end_p = hop_s(top, 1), hop_s(end, -1)
    plan, rowpot, colpot, _, _ = barrier((plan, rowpot, colpot, top, end))
    own, mass = own_call(spots, lat, plan, mass, top_p, end_m)
    rowpot, colpot = rowpot * LN2, colpot * LN2
    own, top_m, end_p, rowpot, colpot = barrier((own, top_m, end_p, rowpot, colpot))
    keep, mass, *parts = sum_call(own, mass, top_m, end_p)
    parts = [hop_f(v, ORDER[k]) for v, k in zip(parts, (3, 2, 1))]
    return finish_call(keep, mass, parts), rowpot, colpot


def eye():
    return lax.broadcasted_iota(jnp.int32, (128, 128), 0) == lax.broadcasted_iota(
        jnp.int32, (128, 128), 1
    )


def to_lanes(column):
    mask = eye()
    return jnp.concatenate(
        [
            jnp.sum(jnp.where(mask, column[at : at + 128], 0.0), axis=0, keepdims=True)
            for at in range(0, column.shape[0], 128)
        ],
        axis=1,
    )


def to_sublanes(line):
    mask = eye()
    return jnp.concatenate(
        [
            jnp.sum(jnp.where(mask, line[:, at : at + 128], 0.0), axis=1, keepdims=True)
            for at in range(0, line.shape[1], 128)
        ],
        axis=0,
    )


TAIL = 16


def pack(mass, lanes):
    high = mass.astype(BF16).astype(F32)
    row = lax.broadcasted_iota(jnp.int32, (TAIL, lanes), 0)
    out = jnp.zeros((TAIL, lanes), F32)
    line = jnp.concatenate([high, mass - high], axis=1)
    for k in range(line.shape[1] // lanes):
        out = jnp.where(row == k, line[:, k * lanes : (k + 1) * lanes], out)
    return out.astype(BF16)


def unpack(tail, count):
    tail = tail.astype(F32)
    line = jnp.concatenate([tail[k : k + 1] for k in range(2 * count // tail.shape[1])], axis=1)
    return line[:, :count] + line[:, count:]


def row_lse_block(read, rows, out):
    step = 32
    columns = []
    for at in range(0, rows, step):
        t = read(at, step)
        high = jnp.max(t, axis=1, keepdims=True)
        total = jnp.sum(jnp.exp2(t - high), axis=1, keepdims=True)
        columns.append(high + jnp.log2(total))
    out[...] = to_lanes(jnp.concatenate(columns, axis=0))


def fetch(quarter, spot_ref, lat_refs, buf, sem):
    width = buf.shape[1] // 4
    for n in range(16):
        spot = spot_ref[n]

        @pl.when(spot // 4 == quarter)
        def start():
            lane = pl.multiple_of(lax.rem(spot, 4) * width, width)
            pltpu.make_async_copy(
                lat_refs[n // 2].at[:, pl.ds(n % 2 * width, width)], buf.at[:, pl.ds(lane, width)], sem
            ).start()


def arrive(buf, sem):
    pltpu.make_async_copy(buf, buf, sem).wait()


def near_kernel(spot_ref, *refs):
    line_refs, near_refs, lat_refs = refs[:4], refs[4:8], refs[8:16]
    cross_ref, last_ref, noise_buf, lat_buf, noise_sem, lat_sem = refs[16:]
    half = cross_ref.shape[0] // 2
    width = line_refs[0].shape[1]

    def start(quarter):
        if quarter == 3:
            fetch(3, spot_ref, lat_refs, last_ref, lat_sem.at[1])
            return
        slot = quarter % 2
        fetch(quarter, spot_ref, lat_refs, lat_buf.at[slot], lat_sem.at[slot])
        for k in range(4):
            lanes = pl.ds(k * width, width)
            if quarter == 0:
                pltpu.make_async_copy(
                    line_refs[k], noise_buf.at[slot, :, lanes], noise_sem.at[slot]
                ).start()
            else:
                for part in range(2):
                    pltpu.make_async_copy(
                        near_refs[2 * quarter - 2 + part].at[k],
                        noise_buf.at[slot, pl.ds(part * half, half), lanes],
                        noise_sem.at[slot],
                    ).start()

    start(0)
    for quarter in range(3):
        slot = quarter % 2
        arrive(noise_buf.at[slot], noise_sem.at[slot])
        arrive(lat_buf.at[slot], lat_sem.at[slot])
        start(quarter + 1)
        cross = lax.dot_general(
            noise_buf[slot], lat_buf[slot], (((1,), (1,)), ((), ())), preferred_element_type=F32
        )
        cross_ref[...] = cross if quarter == 0 else cross_ref[...] + cross
    arrive(last_ref, lat_sem.at[1])


def near_call(spots, line, near, lat):
    rows, width = line[0].shape
    cols = lat[0].shape[0]
    return pl.pallas_call(
        near_kernel,
        in_specs=[pl.BlockSpec(memory_space=pltpu.SMEM)] + [pl.BlockSpec(memory_space=pl.ANY)] * 16,
        out_specs=[pl.BlockSpec(memory_space=pltpu.VMEM)] * 2,
        out_shape=[
            jax.ShapeDtypeStruct((rows, cols), F32),
            jax.ShapeDtypeStruct((cols, 4 * width), BF16),
        ],
        scratch_shapes=[
            pltpu.VMEM((2, rows, 4 * width), BF16),
            pltpu.VMEM((2, cols, 4 * width), BF16),
            pltpu.SemaphoreType.DMA((2,)),
            pltpu.SemaphoreType.DMA((2,)),
        ],
        cost_estimate=pl.CostEstimate(
            flops=2 * rows * cols * 12 * width,
            bytes_accessed=2 * (rows * 12 + cols * 16) * width + 4 * rows * cols,
            transcendentals=0,
        ),
        compiler_params=pltpu.CompilerParams(vmem_limit_bytes=14 * 2**20),
        name="cross_near",
    )(spots, *line, *near, *lat)


def far_kernel(scale, top_ref, end_ref, lat_ref, cross_ref, logits_ref, lse_ref):
    def finish(part_ref):
        noise = jnp.concatenate([part_ref[k] for k in range(4)], axis=1)
        cross = lax.dot_general(
            noise, lat_ref[...], (((1,), (1,)), ((), ())), preferred_element_type=F32
        )
        logits_ref[...] = (cross_ref[...] + cross) * scale

    pl.when(pl.program_id(0) == 0)(lambda: finish(top_ref))
    pl.when(pl.program_id(0) == 1)(lambda: finish(end_ref))
    row_lse_block(lambda at, n: logits_ref[pl.ds(at, n), :], logits_ref.shape[0], lse_ref)


def far_call(far, lat, cross, scale):
    rows, cols = cross.shape
    half, width = far[0].shape[1:]
    return pl.pallas_call(
        functools.partial(far_kernel, scale),
        grid=(2,),
        in_specs=[
            pl.BlockSpec((4, half, width), lambda i: (0, 0, 0)),
            pl.BlockSpec((4, half, width), lambda i: (0, 0, 0)),
            pl.BlockSpec((cols, 4 * width), lambda i: (0, 0)),
            pl.BlockSpec((half, cols), lambda i: (i, 0)),
        ],
        out_specs=[
            pl.BlockSpec((half, cols), lambda i: (i, 0)),
            pl.BlockSpec((1, half), lambda i: (0, i)),
        ],
        out_shape=[
            jax.ShapeDtypeStruct((rows, cols), F32),
            jax.ShapeDtypeStruct((1, rows), F32),
        ],
        cost_estimate=pl.CostEstimate(
            flops=2 * rows * cols * 4 * width,
            bytes_accessed=2 * (rows + cols) * 4 * width + 8 * rows * cols,
            transcendentals=rows * cols,
        ),
        compiler_params=pltpu.CompilerParams(vmem_limit_bytes=24 * 2**20),
        name="cross_far",
    )(*far, lat, cross)


def row_kernel(logits_ref, colpot_ref, lse_ref):
    colpot = colpot_ref[...]
    row_lse_block(
        lambda at, n: logits_ref[pl.ds(at, n), :] + colpot, logits_ref.shape[0], lse_ref
    )


def row_call(logits, colpot):
    rows, cols = logits.shape
    block = 256
    return pl.pallas_call(
        row_kernel,
        grid=(rows // block,),
        in_specs=[
            pl.BlockSpec((block, cols), lambda i: (i, 0)),
            pl.BlockSpec((1, cols), lambda i: (0, 0)),
        ],
        out_specs=pl.BlockSpec((1, block), lambda i: (0, i)),
        out_shape=jax.ShapeDtypeStruct((1, rows), F32),
        compiler_params=pltpu.CompilerParams(vmem_limit_bytes=16 * 2**20),
        name="row_lse",
    )(logits, colpot)


def col_kernel(logits_ref, rowpot_ref, lse_ref, part_ref):
    step = pl.program_id(0)
    rows, cols = logits_ref.shape
    rowpot = jnp.broadcast_to(to_sublanes(rowpot_ref[...]), (rows, 128))
    lines = []
    for at in range(0, cols, 128):
        t = logits_ref[:, pl.ds(at, 128)] + rowpot
        high = jnp.max(t, axis=0, keepdims=True)
        total = jnp.sum(jnp.exp2(t - high), axis=0, keepdims=True)
        lines.append(high + jnp.log2(total))
    part_ref[pl.ds(step, 1), :] = jnp.concatenate(lines, axis=1)

    @pl.when(step == pl.num_programs(0) - 1)
    def finish():
        parts = part_ref[...]
        high = jnp.max(parts, axis=0, keepdims=True)
        total = jnp.sum(jnp.exp2(parts - high), axis=0, keepdims=True)
        lse_ref[...] = high + jnp.log2(total)


def col_call(logits, rowpot):
    rows, cols = logits.shape
    block = 256
    return pl.pallas_call(
        col_kernel,
        grid=(rows // block,),
        in_specs=[
            pl.BlockSpec((block, cols), lambda i: (i, 0)),
            pl.BlockSpec((1, block), lambda i: (0, i)),
        ],
        out_specs=pl.BlockSpec((1, cols), lambda i: (0, 0)),
        out_shape=jax.ShapeDtypeStruct((1, cols), F32),
        scratch_shapes=[pltpu.VMEM((rows // block, cols), F32)],
        compiler_params=pltpu.CompilerParams(vmem_limit_bytes=16 * 2**20),
        name="col_lse",
    )(logits, rowpot)


def plan_kernel(logits_ref, rowpot_ref, colpot_ref, lat_ref, plan_ref, mass_ref, top_ref, end_ref):
    rows = logits_ref.shape[0]
    half = rows // 2
    colpot = colpot_ref[...]
    step = 256
    for at in range(0, rows, step):
        for k in range(at, at + step, 64):
            rowpot = rowpot_ref[:, pl.ds(k // 128 * 128, 128)]
            rowpot = to_sublanes(rowpot)[k % 128 : k % 128 + 64]
            plan_ref[pl.ds(k, 64), :] = jnp.exp2(
                logits_ref[pl.ds(k, 64), :] + rowpot + colpot
            ).astype(BF16)
        mass = jnp.sum(plan_ref[pl.ds(at, step), :].astype(F32), axis=1, keepdims=True)
        mass_ref[:, pl.ds(at, step)] = to_lanes(mass)
        if at + step in (half, rows):
            out_ref = top_ref if at < half else end_ref
            start = at + step - half
            out_ref[:half, :] = jnp.dot(
                plan_ref[pl.ds(start, half), :], lat_ref[...], preferred_element_type=F32
            ).astype(BF16)
            out_ref[half:, :] = pack(mass_ref[:, pl.ds(start, half)], out_ref.shape[1])


def in_vmem(kernel, name, out_shape, flops, *args):
    return pl.pallas_call(
        kernel,
        in_specs=[pl.BlockSpec(memory_space=pltpu.VMEM)] * len(args),
        out_specs=jax.tree.map(lambda _: pl.BlockSpec(memory_space=pltpu.VMEM), out_shape),
        out_shape=out_shape,
        cost_estimate=pl.CostEstimate(
            flops=flops,
            bytes_accessed=sum(a.size * a.dtype.itemsize for a in args),
            transcendentals=0,
        ),
        compiler_params=pltpu.CompilerParams(vmem_limit_bytes=24 * 2**20),
        name=name,
    )(*args)


def plan_call(logits, rowpot, colpot, lat):
    rows, cols = logits.shape
    depth = lat.shape[1]
    share = jax.ShapeDtypeStruct((rows // 2 + TAIL, depth), BF16)
    out_shape = [
        jax.ShapeDtypeStruct((rows, cols), BF16),
        jax.ShapeDtypeStruct((1, rows), F32),
        share,
        share,
    ]
    return in_vmem(
        plan_kernel, "plan", out_shape, 2 * rows * cols * depth, logits, rowpot, colpot, lat
    )


def lat_call(kernel, name, out_shape, flops, spots, lat, scratch, *args):
    space = [pltpu.SMEM] + [pl.ANY] * len(lat) + [pltpu.VMEM] * len(args)
    return pl.pallas_call(
        kernel,
        in_specs=[pl.BlockSpec(memory_space=m) for m in space],
        out_specs=[pl.BlockSpec(memory_space=pltpu.VMEM)] * len(out_shape),
        out_shape=out_shape,
        scratch_shapes=scratch,
        cost_estimate=pl.CostEstimate(
            flops=flops,
            bytes_accessed=sum(a.size * a.dtype.itemsize for a in args),
            transcendentals=0,
        ),
        compiler_params=pltpu.CompilerParams(vmem_limit_bytes=24 * 2**20),
        name=name,
    )(spots, *lat, *args)


def share_kernel(spot_ref, *refs):
    lat_refs, plan_ref, mass_ref = refs[:8], refs[8], refs[9]
    end_ref, top_ref, after_ref, before_ref, sem = refs[10:]
    half = plan_ref.shape[0] // 2
    fetch(1, spot_ref, lat_refs, after_ref, sem.at[0])
    fetch(2, spot_ref, lat_refs, before_ref, sem.at[1])
    for n, (lat_ref, out_ref, rows) in enumerate(
        ((after_ref, end_ref, pl.ds(half, half)), (before_ref, top_ref, pl.ds(0, half)))
    ):
        out_ref[half:, :] = pack(mass_ref[:, rows], out_ref.shape[1])
        arrive(lat_ref, sem.at[n])
        out_ref[:half, :] = jnp.dot(
            plan_ref[rows, :], lat_ref[...], preferred_element_type=F32
        ).astype(BF16)


def share_call(spots, lat, plan, mass):
    rows, cols = plan.shape
    depth = 2 * lat[0].shape[1]
    share = jax.ShapeDtypeStruct((rows // 2 + TAIL, depth), BF16)
    quarter = jax.ShapeDtypeStruct((cols, depth), BF16)
    return lat_call(
        share_kernel, "share", [share, share, quarter, quarter], 2 * rows * cols * depth,
        spots, lat, [pltpu.SemaphoreType.DMA((2,))], plan, mass,
    )


def onward_kernel(plan_ref, after_ref, before_ref, mass_ref, top_more, end_more, top_ref, end_ref):
    half = plan_ref.shape[0] // 2
    for lat_ref, more, rows, out_ref in (
        (after_ref, top_more, pl.ds(0, half), top_ref),
        (before_ref, end_more, pl.ds(half, half), end_ref),
    ):
        share = jnp.dot(plan_ref[rows, :], lat_ref[...], preferred_element_type=F32)
        out_ref[:half, :] = (share + more[:half, :].astype(F32)).astype(BF16)
        out_ref[half:, :] = pack(mass_ref[:, rows] + unpack(more[half:, :], half), out_ref.shape[1])


def onward_call(plan, after, before, mass, top_more, end_more):
    rows, cols = plan.shape
    depth = after.shape[1]
    out_shape = [jax.ShapeDtypeStruct((rows // 2 + TAIL, depth), BF16)] * 2
    return in_vmem(
        onward_kernel, "onward", out_shape, 2 * rows * cols * depth,
        plan, after, before, mass, top_more, end_more,
    )


def sum_kernel(own_ref, mass_ref, top_ref, end_ref, keep_ref, total_ref, *part_refs):
    rows = own_ref.shape[0]
    half, width = rows // 2, keep_ref.shape[1]
    for start, more in ((0, top_ref), (half, end_ref)):
        there = pl.ds(start, half)
        total_ref[:, there] = mass_ref[:, there] + unpack(more[half:, :], half)
    tail = pack(total_ref[...], width)
    step = 128
    for k, out_ref in zip((3, 2, 1, 0), (*part_refs, keep_ref)):
        lanes = pl.ds(k * width, width)
        for start, more in ((0, top_ref), (half, end_ref)):
            for at in range(0, half, step):
                there = pl.ds(start + at, step)
                value = own_ref[there, lanes] + more[pl.ds(at, step), lanes].astype(F32)
                out_ref[there, :] = value.astype(out_ref.dtype)
        if k:
            out_ref[rows:, :] = tail


def sum_call(own, mass, *received):
    rows, depth = own.shape
    width = depth // 4
    part = jax.ShapeDtypeStruct((rows + TAIL, width), BF16)
    out_shape = [
        jax.ShapeDtypeStruct((rows, width), F32),
        jax.ShapeDtypeStruct((1, rows), F32),
        part, part, part,
    ]
    return in_vmem(sum_kernel, "sum_s", out_shape, 2 * rows * depth, own, mass, *received)


def finish_kernel(keep_ref, mass_ref, *refs):
    part_refs, out_ref = refs[:-1], refs[-1]
    rows = keep_ref.shape[0]
    mass = mass_ref[...]
    for part in part_refs:
        mass = mass + unpack(part[rows:, :], rows)
    step = 128
    for at in range(0, rows, step):
        there = pl.ds(at, step)
        value = keep_ref[there, :]
        for part in part_refs:
            value = value + part[there, :].astype(F32)
        out_ref[there, :] = (value / to_sublanes(mass[:, at : at + step])).astype(BF16)


def finish_call(keep, mass, parts):
    out_shape = [jax.ShapeDtypeStruct(keep.shape, BF16)]
    return in_vmem(finish_kernel, "finish", out_shape, 4 * keep.size, keep, mass, *parts)[0]


def own_kernel(spot_ref, *refs):
    lat_refs, (plan_ref, mass_ref, top_ref, end_ref) = refs[:8], refs[8:12]
    out_ref, total_ref, lat_buf, sem = refs[12:]
    half = plan_ref.shape[0] // 2
    fetch(0, spot_ref, lat_refs, lat_buf, sem)
    arrive(lat_buf, sem)
    for rows, more in ((pl.ds(0, half), top_ref), (pl.ds(half, half), end_ref)):
        share = jnp.dot(plan_ref[rows, :], lat_buf[...], preferred_element_type=F32)
        out_ref[rows, :] = share + more[:half, :].astype(F32)
        total_ref[:, rows] = mass_ref[:, rows] + unpack(more[half:, :], half)


def own_call(spots, lat, plan, mass, top, end):
    rows, cols = plan.shape
    depth = 2 * lat[0].shape[1]
    return lat_call(
        own_kernel,
        "own",
        [jax.ShapeDtypeStruct((rows, depth), F32), jax.ShapeDtypeStruct((1, rows), F32)],
        2 * rows * cols * depth,
        spots, lat, [pltpu.VMEM((cols, depth), BF16), pltpu.SemaphoreType.DMA],
        plan, mass, top, end,
    )


def on_device(noise, latents):
    width = latents.shape[1] * lax.axis_size("row")
    noise_count = noise.shape[0] * lax.axis_size("row")
    latent_count = latents.shape[0] * lax.axis_size("col")
    line, near, far, pieces = gather(noise, latents)
    spots = latent_spots()
    cross, last = near_call(spots, line, near, pieces)
    logits, lse = far_call(far, last, cross, 2.0 / (width * EPSILON) * LOG2E)
    for step in range(ITERS):
        if step:
            lse = row_call(logits, colpot)
        rowpot = -math.log2(noise_count) - over_col(lse, logadd)
        colpot = -math.log2(latent_count) - over_row(col_call(logits, rowpot), logadd)
    plan, mass, far_top, far_end = plan_call(logits, rowpot, colpot, last)
    transported, rowpot, colpot = scatter_sum(
        plan, spots, pieces, far_top, far_end, mass, rowpot, colpot
    )
    return (transported, rowpot.reshape(-1), colpot.reshape(-1))


def solution(mesh):
    in_specs = (P("row", "col"), P("col", "row"))
    out_specs = (P("row", "col"), P("row"), P("col"))
    return jax.shard_map(
        on_device, mesh=mesh, in_specs=in_specs, out_specs=out_specs, check_vma=False
    )
```

```python
import functools
import math

import jax
import jax.numpy as jnp
from jax import lax
from jax.experimental import pallas as pl
from jax.experimental.pallas import tpu as pltpu
from jax.sharding import PartitionSpec as P

ITERS = 3
EPSILON = 0.01
LOG2E = math.log2(math.e)
LN2 = math.log(2.0)
NX, NY, NZ, NC = 4, 4, 4, 2

F32 = jnp.float32
BF16 = jnp.bfloat16


def shift_z(by):
    return [(x * NZ + z, x * NZ + (z + by) % NZ) for x in range(NX) for z in range(NZ)]


def shift_x(by):
    return [(x * NZ + z, (x + by) % NX * NZ + z) for x in range(NX) for z in range(NZ)]


def shift_y(by):
    return [(y * NC + c, (y + by) % NY * NC + c) for y in range(NY) for c in range(NC)]


def swap_core():
    return [(y * NC + c, y * NC + 1 - c) for y in range(NY) for c in range(NC)]


def logadd(parts):
    high = functools.reduce(jnp.maximum, parts)
    total = functools.reduce(jnp.add, [jnp.exp2(p - high) for p in parts])
    return high + jnp.log2(total)


BOTH = ("row", "col")


def spread_y():
    return [
        (y * NC + c, (y + 1 - 2 * c) % NY * NC + c) for y in range(NY) for c in range(NC)
    ]


def everywhere(perms):
    count = NX * NZ
    return [
        (row * count + a, row * count + b) for row in range(NY * NC) for a, b in perms[row % NC]
    ]


def around(value, axis, spread, opposite, combine):
    far = lax.ppermute(value, axis, opposite)
    near = lax.ppermute(value, axis, spread)
    return combine([value, far, near, lax.ppermute(near, "row", swap_core())])


def over_col(value, combine):
    mine = lax.axis_index("row") % NC == 0
    other = lax.ppermute(value, "row", swap_core())
    both = jnp.concatenate(
        [jnp.where(mine, value, other), jnp.where(mine, other, value)], axis=0
    )
    for shift in (shift_z, shift_x):
        both = around(both, BOTH, everywhere([shift(1), shift(-1)]), everywhere([shift(2)] * 2), combine)
    return jnp.where(mine, both[:1], both[1:])


def over_row(value, combine):
    value = combine([value, lax.ppermute(value, "row", swap_core())])
    return around(value, "row", spread_y(), shift_y(2), combine)


ORDER = (0, 1, 3, 2)


def hop_f(value, by):
    return lax.ppermute(value, BOTH, everywhere([shift_z(by), shift_x(by)]))


def hop_s(value, by):
    return lax.ppermute(value, BOTH, everywhere([shift_x(by), shift_z(by)]))


def gather(noise, latents):
    rows, width = noise.shape
    half = rows // 2
    swap = lambda v: lax.ppermute(v, "row", swap_core())
    opposite = hop_f(noise, 2)
    line = [noise, hop_f(noise, -1), hop_f(noise, 1), opposite]
    near = lax.ppermute(latents, "row", spread_y())
    away = lax.ppermute(latents, "row", [(b, a) for a, b in spread_y()])
    top, end = halves_call(line)
    after, _, _ = lax.optimization_barrier((near, top, end))
    top_m, end_p = hop_s(top, 1), hop_s(end, -1)
    end_m, top_p = hop_s(end, 1), hop_s(top, -1)
    far = lax.ppermute(after, "row", spread_y())
    first, last, other = lax.optimization_barrier((top_m, end_p, swap(latents)))
    top_far, end_far = hop_s(first, 1), hop_s(last, -1)
    end_m, top_p, here, there = lax.optimization_barrier((end_m, top_p, near, away))
    near_other, away_other = swap(here), swap(there)
    split = lambda v: v.reshape(4, half, width)
    lat = [latents, other, near, near_other, away, away_other, far, swap(far)]
    return (
        line,
        [split(v) for v in (top_p, end_p, top_m, end_m)],
        [split(top_far), split(end_far)],
        lat,
    )


def latent_spots():
    row, col = lax.axis_index("row"), lax.axis_index("col")
    y, core = row // NC, row % NC
    block = lambda dy, flip: (y + dy) % NY * NC + (core if not flip else 1 - core)
    back = jnp.where(core == 0, 3, 1)
    rows = [
        block(0, False), block(0, True), block(back, False), block(4 - back, True),
        block(4 - back, False), block(back, True), block(2, False), block(2, True),
    ]
    at = (jnp.stack(rows)[:, None] * 2 + jnp.arange(2)[None, :]).reshape(-1)
    dx, dz = (at // NZ - col // NZ) % NX, (at % NZ - col % NZ) % NZ
    df, ds = jnp.where(core == 0, dz, dx), jnp.where(core == 0, dx, dz)
    rank = lambda d: jnp.where(d < 2, d, 5 - d)
    return (rank(ds) * 4 + rank(df)).astype(jnp.int32)


def scatter_sum(plan, spots, lat, far_top, far_end, mass, rowpot, colpot):
    barrier = lax.optimization_barrier
    far_top, far_end = hop_s(far_top, 1), hop_s(far_end, -1)
    end, top, after, before = share_call(spots, lat, plan, mass)
    end_m, top_p = hop_s(end, 1), hop_s(top, -1)
    top, end = onward_call(plan, after, before, mass, far_top, far_end)
    top_m, end_p = hop_s(top, 1), hop_s(end, -1)
    plan, rowpot, colpot, _, _ = barrier((plan, rowpot, colpot, top, end))
    own, mass = own_call(spots, lat, plan, mass, top_p, end_m)
    rowpot, colpot = rowpot * LN2, colpot * LN2
    own, top_m, end_p, rowpot, colpot = barrier((own, top_m, end_p, rowpot, colpot))
    keep, mass, *parts = sum_call(own, mass, top_m, end_p)
    parts = [hop_f(v, ORDER[k]) for v, k in zip(parts, (3, 2, 1))]
    return finish_call(keep, mass, parts).astype(BF16), rowpot, colpot


def eye():
    return lax.broadcasted_iota(jnp.int32, (128, 128), 0) == lax.broadcasted_iota(
        jnp.int32, (128, 128), 1
    )


def to_lanes(column):
    mask = eye()
    return jnp.concatenate(
        [
            jnp.sum(jnp.where(mask, column[at : at + 128], 0.0), axis=0, keepdims=True)
            for at in range(0, column.shape[0], 128)
        ],
        axis=1,
    )


def to_sublanes(line):
    mask = eye()
    return jnp.concatenate(
        [
            jnp.sum(jnp.where(mask, line[:, at : at + 128], 0.0), axis=1, keepdims=True)
            for at in range(0, line.shape[1], 128)
        ],
        axis=0,
    )


TAIL = 16


def pack(mass, lanes):
    high = mass.astype(BF16).astype(F32)
    row = lax.broadcasted_iota(jnp.int32, (TAIL, lanes), 0)
    out = jnp.zeros((TAIL, lanes), F32)
    line = jnp.concatenate([high, mass - high], axis=1)
    for k in range(line.shape[1] // lanes):
        out = jnp.where(row == k, line[:, k * lanes : (k + 1) * lanes], out)
    return out.astype(BF16)


def unpack(tail, count):
    tail = tail.astype(F32)
    line = jnp.concatenate([tail[k : k + 1] for k in range(2 * count // tail.shape[1])], axis=1)
    return line[:, :count] + line[:, count:]


def row_lse_block(read, rows, out):
    step = 32
    columns = []
    for at in range(0, rows, step):
        t = read(at, step)
        high = jnp.max(t, axis=1, keepdims=True)
        total = jnp.sum(jnp.exp2(t - high), axis=1, keepdims=True)
        columns.append(high + jnp.log2(total))
    out[...] = to_lanes(jnp.concatenate(columns, axis=0))


def halves_kernel(*refs):
    blocks, outs, sem = refs[:4], refs[4:6], refs[6]
    half = blocks[0].shape[0] // 2
    copies = [
        pltpu.make_async_copy(
            block.at[pl.ds(part * half, half), :], out.at[pl.ds(k * half, half), :], sem.at[part, k]
        )
        for part, out in enumerate(outs)
        for k, block in enumerate(blocks)
    ]
    for copy in copies:
        copy.start()
    for copy in copies:
        copy.wait()


def halves_call(blocks):
    rows, width = blocks[0].shape
    return pl.pallas_call(
        halves_kernel,
        in_specs=[pl.BlockSpec(memory_space=pl.ANY)] * 4,
        out_specs=[pl.BlockSpec(memory_space=pl.ANY)] * 2,
        out_shape=[jax.ShapeDtypeStruct((2 * rows, width), BF16)] * 2,
        scratch_shapes=[pltpu.SemaphoreType.DMA((2, 4))],
        cost_estimate=pl.CostEstimate(
            flops=0, bytes_accessed=16 * rows * width, transcendentals=0
        ),
        compiler_params=pltpu.CompilerParams(vmem_limit_bytes=2 * 2**20),
        name="halves",
    )(*blocks)


def fetch(quarter, spot_ref, lat_refs, buf, sem):
    width = buf.shape[1] // 4
    for n in range(16):
        spot = spot_ref[n]

        @pl.when(spot // 4 == quarter)
        def start():
            lane = pl.multiple_of(lax.rem(spot, 4) * width, width)
            pltpu.make_async_copy(
                lat_refs[n // 2].at[:, pl.ds(n % 2 * width, width)], buf.at[:, pl.ds(lane, width)], sem
            ).start()


def arrive(buf, sem):
    pltpu.make_async_copy(buf, buf, sem).wait()


def near_kernel(spot_ref, *refs):
    line_refs, near_refs, lat_refs = refs[:4], refs[4:8], refs[8:16]
    cross_ref, last_ref, noise_buf, lat_buf, noise_sem, lat_sem = refs[16:]
    half = cross_ref.shape[0] // 2
    width = line_refs[0].shape[1]

    def start(quarter):
        if quarter == 3:
            fetch(3, spot_ref, lat_refs, last_ref, lat_sem.at[1])
            return
        slot = quarter % 2
        fetch(quarter, spot_ref, lat_refs, lat_buf.at[slot], lat_sem.at[slot])
        for k in range(4):
            lanes = pl.ds(k * width, width)
            if quarter == 0:
                pltpu.make_async_copy(
                    line_refs[k], noise_buf.at[slot, :, lanes], noise_sem.at[slot]
                ).start()
            else:
                for part in range(2):
                    pltpu.make_async_copy(
                        near_refs[2 * quarter - 2 + part].at[k],
                        noise_buf.at[slot, pl.ds(part * half, half), lanes],
                        noise_sem.at[slot],
                    ).start()

    start(0)
    for quarter in range(3):
        slot = quarter % 2
        arrive(noise_buf.at[slot], noise_sem.at[slot])
        arrive(lat_buf.at[slot], lat_sem.at[slot])
        start(quarter + 1)
        cross = lax.dot_general(
            noise_buf[slot], lat_buf[slot], (((1,), (1,)), ((), ())), preferred_element_type=F32
        )
        cross_ref[...] = cross if quarter == 0 else cross_ref[...] + cross
    arrive(last_ref, lat_sem.at[1])


def in_hbm(value):
    return pltpu.with_memory_space_constraint(value, pltpu.HBM)


def near_call(spots, line, near, lat):
    rows, width = line[0].shape
    cols = lat[0].shape[0]
    return pl.pallas_call(
        near_kernel,
        in_specs=[pl.BlockSpec(memory_space=pltpu.SMEM)] + [pl.BlockSpec(memory_space=pl.ANY)] * 16,
        out_specs=[pl.BlockSpec(memory_space=pltpu.VMEM)] * 2,
        out_shape=[
            jax.ShapeDtypeStruct((rows, cols), F32),
            jax.ShapeDtypeStruct((cols, 4 * width), BF16),
        ],
        scratch_shapes=[
            pltpu.VMEM((2, rows, 4 * width), BF16),
            pltpu.VMEM((2, cols, 4 * width), BF16),
            pltpu.SemaphoreType.DMA((2,)),
            pltpu.SemaphoreType.DMA((2,)),
        ],
        cost_estimate=pl.CostEstimate(
            flops=8 * rows * cols * 12 * width,
            bytes_accessed=2 * (rows * 12 + cols * 16) * width + 4 * rows * cols,
            transcendentals=0,
        ),
        compiler_params=pltpu.CompilerParams(vmem_limit_bytes=14 * 2**20),
        name="cross_near",
    )(spots, *[in_hbm(v) for v in (*line, *near)], *[v if k % 2 else in_hbm(v) for k, v in enumerate(lat)])


def far_kernel(scale, top_ref, end_ref, lat_ref, cross_ref, logits_ref, lse_ref):
    half = top_ref.shape[1]
    block = 256
    for start, part_ref in ((0, top_ref), (half, end_ref)):
        rows = pl.ds(start, half)
        noise = jnp.concatenate([part_ref[k] for k in range(4)], axis=1)
        cross = lax.dot_general(
            noise, lat_ref[...], (((1,), (1,)), ((), ())), preferred_element_type=F32
        )
        logits_ref[rows, :] = (cross_ref[rows, :] + cross) * scale
        for at in range(start, start + half, block):
            row_lse_block(
                lambda k, n: logits_ref[pl.ds(at + k, n), :], block, lse_ref.at[:, pl.ds(at, block)]
            )


def far_call(far, lat, cross, scale):
    rows, cols = cross.shape
    out_shape = [
        jax.ShapeDtypeStruct((rows, cols), F32),
        jax.ShapeDtypeStruct((1, rows), F32),
    ]
    return in_vmem(
        functools.partial(far_kernel, scale), "cross_far", out_shape,
        2 * rows * cols * lat.shape[1], *far, lat, cross,
    )


def row_kernel(logits_ref, colpot_ref, lse_ref):
    colpot = colpot_ref[...]
    block = 256

    def some_rows(i, _):
        first = pl.multiple_of(i * block, block)
        row_lse_block(
            lambda at, n: logits_ref[pl.ds(first + at, n), :] + colpot,
            block,
            lse_ref.at[:, pl.ds(first, block)],
        )
        return 0

    lax.fori_loop(0, logits_ref.shape[0] // block, some_rows, 0)


def row_call(logits, colpot):
    out_shape = [jax.ShapeDtypeStruct((1, logits.shape[0]), F32)]
    return in_vmem(row_kernel, "row_lse", out_shape, 8 * logits.size, logits, colpot)[0]


def col_kernel(logits_ref, rowpot_ref, lse_ref):
    rows, cols = logits_ref.shape
    block = 256

    def some_rows(i, parts):
        first = pl.multiple_of(i * block, block)
        rowpot = to_sublanes(rowpot_ref[:, pl.ds(first, block)])
        rowpot = jnp.broadcast_to(rowpot, (block, 128))
        lines = []
        for at in range(0, cols, 128):
            t = logits_ref[pl.ds(first, block), pl.ds(at, 128)] + rowpot
            high = jnp.max(t, axis=0, keepdims=True)
            total = jnp.sum(jnp.exp2(t - high), axis=0, keepdims=True)
            lines.append(high + jnp.log2(total))
        part = jnp.concatenate(lines, axis=1)
        row = lax.broadcasted_iota(jnp.int32, parts.shape, 0)
        return jnp.where(row == i, part, parts)

    parts = lax.fori_loop(
        0, rows // block, some_rows, jnp.full((rows // block, cols), -jnp.inf, F32)
    )
    high = jnp.max(parts, axis=0, keepdims=True)
    lse_ref[...] = high + jnp.log2(jnp.sum(jnp.exp2(parts - high), axis=0, keepdims=True))


def col_call(logits, rowpot):
    out_shape = [jax.ShapeDtypeStruct((1, logits.shape[1]), F32)]
    return in_vmem(col_kernel, "col_lse", out_shape, 8 * logits.size, logits, rowpot)[0]


def plan_kernel(logits_ref, rowpot_ref, colpot_ref, lat_ref, plan_ref, mass_ref, top_ref, end_ref):
    rows = logits_ref.shape[0]
    half = rows // 2
    colpot = colpot_ref[...]
    step = 256
    for at in range(0, rows, step):
        for k in range(at, at + step, 64):
            rowpot = rowpot_ref[:, pl.ds(k // 128 * 128, 128)]
            rowpot = to_sublanes(rowpot)[k % 128 : k % 128 + 64]
            plan_ref[pl.ds(k, 64), :] = jnp.exp2(
                logits_ref[pl.ds(k, 64), :] + rowpot + colpot
            ).astype(BF16)
        mass = jnp.sum(plan_ref[pl.ds(at, step), :].astype(F32), axis=1, keepdims=True)
        mass_ref[:, pl.ds(at, step)] = to_lanes(mass)
        if at + step in (half, rows):
            out_ref = top_ref if at < half else end_ref
            start = at + step - half
            out_ref[:half, :] = jnp.dot(
                plan_ref[pl.ds(start, half), :], lat_ref[...], preferred_element_type=F32
            ).astype(BF16)
            out_ref[half:, :] = pack(mass_ref[:, pl.ds(start, half)], out_ref.shape[1])


def in_vmem(kernel, name, out_shape, flops, *args):
    return pl.pallas_call(
        kernel,
        in_specs=[pl.BlockSpec(memory_space=pltpu.VMEM)] * len(args),
        out_specs=jax.tree.map(lambda _: pl.BlockSpec(memory_space=pltpu.VMEM), out_shape),
        out_shape=out_shape,
        cost_estimate=pl.CostEstimate(
            flops=flops,
            bytes_accessed=sum(a.size * a.dtype.itemsize for a in args),
            transcendentals=0,
        ),
        compiler_params=pltpu.CompilerParams(vmem_limit_bytes=24 * 2**20),
        name=name,
    )(*args)


def plan_call(logits, rowpot, colpot, lat):
    rows, cols = logits.shape
    depth = lat.shape[1]
    share = jax.ShapeDtypeStruct((rows // 2 + TAIL, depth), BF16)
    out_shape = [
        jax.ShapeDtypeStruct((rows, cols), BF16),
        jax.ShapeDtypeStruct((1, rows), F32),
        share,
        share,
    ]
    return in_vmem(
        plan_kernel, "plan", out_shape, 2 * rows * cols * depth, logits, rowpot, colpot, lat
    )


def lat_call(kernel, name, out_shape, flops, spots, lat, scratch, *args):
    space = [pltpu.SMEM] + [pl.ANY] * len(lat) + [pltpu.VMEM] * len(args)
    return pl.pallas_call(
        kernel,
        in_specs=[pl.BlockSpec(memory_space=m) for m in space],
        out_specs=[pl.BlockSpec(memory_space=pltpu.VMEM)] * len(out_shape),
        out_shape=out_shape,
        scratch_shapes=scratch,
        cost_estimate=pl.CostEstimate(
            flops=flops,
            bytes_accessed=sum(a.size * a.dtype.itemsize for a in args),
            transcendentals=0,
        ),
        compiler_params=pltpu.CompilerParams(vmem_limit_bytes=24 * 2**20),
        name=name,
    )(spots, *lat, *args)


def share_kernel(spot_ref, *refs):
    lat_refs, plan_ref, mass_ref = refs[:8], refs[8], refs[9]
    end_ref, top_ref, after_ref, before_ref, sem = refs[10:]
    half = plan_ref.shape[0] // 2
    fetch(1, spot_ref, lat_refs, after_ref, sem.at[0])
    fetch(2, spot_ref, lat_refs, before_ref, sem.at[1])
    for n, (lat_ref, out_ref, rows) in enumerate(
        ((after_ref, end_ref, pl.ds(half, half)), (before_ref, top_ref, pl.ds(0, half)))
    ):
        out_ref[half:, :] = pack(mass_ref[:, rows], out_ref.shape[1])
        arrive(lat_ref, sem.at[n])
        out_ref[:half, :] = jnp.dot(
            plan_ref[rows, :], lat_ref[...], preferred_element_type=F32
        ).astype(BF16)


def share_call(spots, lat, plan, mass):
    rows, cols = plan.shape
    depth = 2 * lat[0].shape[1]
    share = jax.ShapeDtypeStruct((rows // 2 + TAIL, depth), BF16)
    quarter = jax.ShapeDtypeStruct((cols, depth), BF16)
    return lat_call(
        share_kernel, "share", [share, share, quarter, quarter], 2 * rows * cols * depth,
        spots, lat, [pltpu.SemaphoreType.DMA((2,))], plan, mass,
    )


def onward_kernel(plan_ref, after_ref, before_ref, mass_ref, top_more, end_more, top_ref, end_ref):
    half = plan_ref.shape[0] // 2
    for lat_ref, more, rows, out_ref in (
        (after_ref, top_more, pl.ds(0, half), top_ref),
        (before_ref, end_more, pl.ds(half, half), end_ref),
    ):
        share = jnp.dot(plan_ref[rows, :], lat_ref[...], preferred_element_type=F32)
        out_ref[:half, :] = (share + more[:half, :].astype(F32)).astype(BF16)
        out_ref[half:, :] = pack(mass_ref[:, rows] + unpack(more[half:, :], half), out_ref.shape[1])


def onward_call(plan, after, before, mass, top_more, end_more):
    rows, cols = plan.shape
    depth = after.shape[1]
    out_shape = [jax.ShapeDtypeStruct((rows // 2 + TAIL, depth), BF16)] * 2
    return in_vmem(
        onward_kernel, "onward", out_shape, 2 * rows * cols * depth,
        plan, after, before, mass, top_more, end_more,
    )


def sum_kernel(own_ref, mass_ref, top_ref, end_ref, keep_ref, total_ref, *part_refs):
    rows = own_ref.shape[0]
    half, width = rows // 2, keep_ref.shape[1]
    for start, more in ((0, top_ref), (half, end_ref)):
        there = pl.ds(start, half)
        total_ref[:, there] = mass_ref[:, there] + unpack(more[half:, :], half)
    tail = pack(total_ref[...], width)
    step = 128
    for k, out_ref in zip((3, 2, 1, 0), (*part_refs, keep_ref)):
        lanes = pl.ds(k * width, width)
        for start, more in ((0, top_ref), (half, end_ref)):
            for at in range(0, half, step):
                there = pl.ds(start + at, step)
                value = own_ref[there, lanes] + more[pl.ds(at, step), lanes].astype(F32)
                out_ref[there, :] = value.astype(out_ref.dtype)
        if k:
            out_ref[rows:, :] = tail


def sum_call(own, mass, *received):
    rows, depth = own.shape
    width = depth // 4
    part = jax.ShapeDtypeStruct((rows + TAIL, width), BF16)
    out_shape = [
        jax.ShapeDtypeStruct((rows, width), F32),
        jax.ShapeDtypeStruct((1, rows), F32),
        part, part, part,
    ]
    return in_vmem(sum_kernel, "sum_s", out_shape, 2 * rows * depth, own, mass, *received)


def finish_kernel(keep_ref, mass_ref, *refs):
    part_refs, out_ref = refs[:-1], refs[-1]
    rows = keep_ref.shape[0]
    mass = mass_ref[...]
    for part in part_refs:
        mass = mass + unpack(part[rows:, :], rows)
    step = 128
    for at in range(0, rows, step):
        there = pl.ds(at, step)
        value = keep_ref[there, :]
        for part in part_refs:
            value = value + part[there, :].astype(F32)
        out_ref[there, :] = value / to_sublanes(mass[:, at : at + step])


def finish_call(keep, mass, parts):
    out_shape = [jax.ShapeDtypeStruct(keep.shape, F32)]
    return in_vmem(finish_kernel, "finish", out_shape, 4 * keep.size, keep, mass, *parts)[0]


def own_kernel(spot_ref, *refs):
    lat_refs, (plan_ref, mass_ref, top_ref, end_ref) = refs[:8], refs[8:12]
    out_ref, total_ref, lat_buf, sem = refs[12:]
    half = plan_ref.shape[0] // 2
    fetch(0, spot_ref, lat_refs, lat_buf, sem)
    arrive(lat_buf, sem)
    for rows, more in ((pl.ds(0, half), top_ref), (pl.ds(half, half), end_ref)):
        share = jnp.dot(plan_ref[rows, :], lat_buf[...], preferred_element_type=F32)
        out_ref[rows, :] = share + more[:half, :].astype(F32)
        total_ref[:, rows] = mass_ref[:, rows] + unpack(more[half:, :], half)


def own_call(spots, lat, plan, mass, top, end):
    rows, cols = plan.shape
    depth = 2 * lat[0].shape[1]
    return lat_call(
        own_kernel,
        "own",
        [jax.ShapeDtypeStruct((rows, depth), F32), jax.ShapeDtypeStruct((1, rows), F32)],
        2 * rows * cols * depth,
        spots, lat, [pltpu.VMEM((cols, depth), BF16), pltpu.SemaphoreType.DMA],
        plan, mass, top, end,
    )


def on_device(noise, latents):
    width = latents.shape[1] * lax.axis_size("row")
    noise_count = noise.shape[0] * lax.axis_size("row")
    latent_count = latents.shape[0] * lax.axis_size("col")
    line, near, far, pieces = gather(noise, latents)
    spots = latent_spots()
    cross, last = near_call(spots, line, near, pieces)
    logits, lse = far_call(far, last, cross, 2.0 / (width * EPSILON) * LOG2E)
    for step in range(ITERS):
        if step:
            lse = row_call(logits, colpot)
        rowpot = -math.log2(noise_count) - over_col(lse, logadd)
        colpot = -math.log2(latent_count) - over_row(col_call(logits, rowpot), logadd)
    plan, mass, far_top, far_end = plan_call(logits, rowpot, colpot, last)
    transported, rowpot, colpot = scatter_sum(
        plan, spots, pieces, far_top, far_end, mass, rowpot, colpot
    )
    return (transported, rowpot.reshape(-1), colpot.reshape(-1))


def solution(mesh):
    in_specs = (P("row", "col"), P("col", "row"))
    out_specs = (P("row", "col"), P("row"), P("col"))
    return jax.shard_map(
        on_device, mesh=mesh, in_specs=in_specs, out_specs=out_specs, check_vma=False
    )
```

```python
import functools
import math

import jax
import jax.numpy as jnp
from jax import lax
from jax.experimental import pallas as pl
from jax.experimental.pallas import tpu as pltpu
from jax.sharding import PartitionSpec as P

ITERS = 3
EPSILON = 0.01
LOG2E = math.log2(math.e)
LN2 = math.log(2.0)
NX, NY, NZ, NC = 4, 4, 4, 2

F32 = jnp.float32
BF16 = jnp.bfloat16


def shift_z(by):
    return [(x * NZ + z, x * NZ + (z + by) % NZ) for x in range(NX) for z in range(NZ)]


def shift_x(by):
    return [(x * NZ + z, (x + by) % NX * NZ + z) for x in range(NX) for z in range(NZ)]


def shift_y(by):
    return [(y * NC + c, (y + by) % NY * NC + c) for y in range(NY) for c in range(NC)]


def swap_core():
    return [(y * NC + c, y * NC + 1 - c) for y in range(NY) for c in range(NC)]


def logadd(parts):
    high = functools.reduce(jnp.maximum, parts)
    total = functools.reduce(jnp.add, [jnp.exp2(p - high) for p in parts])
    return high + jnp.log2(total)


BOTH = ("row", "col")


def spread_y():
    return [
        (y * NC + c, (y + 1 - 2 * c) % NY * NC + c) for y in range(NY) for c in range(NC)
    ]


def everywhere(perms):
    count = NX * NZ
    return [
        (row * count + a, row * count + b) for row in range(NY * NC) for a, b in perms[row % NC]
    ]


def around(value, axis, spread, opposite, combine):
    far = lax.ppermute(value, axis, opposite)
    near = lax.ppermute(value, axis, spread)
    return combine([value, far, near, lax.ppermute(near, "row", swap_core())])


def over_col(value, combine):
    mine = lax.axis_index("row") % NC == 0
    other = lax.ppermute(value, "row", swap_core())
    both = jnp.concatenate(
        [jnp.where(mine, value, other), jnp.where(mine, other, value)], axis=0
    )
    for shift in (shift_z, shift_x):
        both = around(both, BOTH, everywhere([shift(1), shift(-1)]), everywhere([shift(2)] * 2), combine)
    return jnp.where(mine, both[:1], both[1:])


def over_row(value, combine):
    value = combine([value, lax.ppermute(value, "row", swap_core())])
    return around(value, "row", spread_y(), shift_y(2), combine)


ORDER = (0, 1, 3, 2)


def hop_f(value, by):
    return lax.ppermute(value, BOTH, everywhere([shift_z(by), shift_x(by)]))


def hop_s(value, by):
    return lax.ppermute(value, BOTH, everywhere([shift_x(by), shift_z(by)]))


def gather(noise, latents):
    rows, width = noise.shape
    half = rows // 2
    swap = lambda v: lax.ppermute(v, "row", swap_core())
    opposite = hop_f(noise, 2)
    line = [noise, hop_f(noise, -1), hop_f(noise, 1), opposite]
    near = lax.ppermute(latents, "row", spread_y())
    away = lax.ppermute(latents, "row", [(b, a) for a, b in spread_y()])
    top, end = halves_call(line)
    after, _, _ = lax.optimization_barrier((near, top, end))
    top_m, end_p = hop_s(top, 1), hop_s(end, -1)
    end_m, top_p = hop_s(end, 1), hop_s(top, -1)
    far = lax.ppermute(after, "row", spread_y())
    first, last, other = lax.optimization_barrier((top_m, end_p, swap(latents)))
    top_far, end_far = hop_s(first, 1), hop_s(last, -1)
    end_m, top_p, here, there = lax.optimization_barrier((end_m, top_p, near, away))
    near_other, away_other = swap(here), swap(there)
    split = lambda v: v.reshape(4, half, width)
    lat = [latents, other, near, near_other, away, away_other, far, swap(far)]
    return (
        line,
        [split(v) for v in (top_p, end_p, top_m, end_m)],
        [split(top_far), split(end_far)],
        lat,
    )


def latent_spots():
    row, col = lax.axis_index("row"), lax.axis_index("col")
    y, core = row // NC, row % NC
    block = lambda dy, flip: (y + dy) % NY * NC + (core if not flip else 1 - core)
    back = jnp.where(core == 0, 3, 1)
    rows = [
        block(0, False), block(0, True), block(back, False), block(4 - back, True),
        block(4 - back, False), block(back, True), block(2, False), block(2, True),
    ]
    at = (jnp.stack(rows)[:, None] * 2 + jnp.arange(2)[None, :]).reshape(-1)
    dx, dz = (at // NZ - col // NZ) % NX, (at % NZ - col % NZ) % NZ
    df, ds = jnp.where(core == 0, dz, dx), jnp.where(core == 0, dx, dz)
    rank = lambda d: jnp.where(d < 2, d, 5 - d)
    return (rank(ds) * 4 + rank(df)).astype(jnp.int32)


def scatter_sum(plan, spots, lat, far_top, far_end, mass, rowpot, colpot):
    barrier = lax.optimization_barrier
    far_top, far_end = hop_s(far_top, 1), hop_s(far_end, -1)
    end, top, after, before = share_call(spots, lat, plan, mass)
    end_m, top_p = hop_s(end, 1), hop_s(top, -1)
    top, end = onward_call(plan, after, before, mass, far_top, far_end)
    top_m, end_p = hop_s(top, 1), hop_s(end, -1)
    plan, rowpot, colpot, _, _ = barrier((plan, rowpot, colpot, top, end))
    own, mass = own_call(spots, lat, plan, mass, top_p, end_m)
    rowpot, colpot = rowpot * LN2, colpot * LN2
    own, top_m, end_p, rowpot, colpot = barrier((own, top_m, end_p, rowpot, colpot))
    keep, mass, *parts = sum_call(own, mass, top_m, end_p)
    parts = [hop_f(v, ORDER[k]) for v, k in zip(parts, (3, 2, 1))]
    return finish_call(keep, mass, parts).astype(BF16), rowpot, colpot


def steps_of(total, step, body):
    def turn(i, _):
        body(pl.ds(pl.multiple_of(i * step, step), step))
        return 0

    lax.fori_loop(0, total // step, turn, 0)


def eye():
    return lax.broadcasted_iota(jnp.int32, (128, 128), 0) == lax.broadcasted_iota(
        jnp.int32, (128, 128), 1
    )


def to_lanes(column):
    mask = eye()
    return jnp.concatenate(
        [
            jnp.sum(jnp.where(mask, column[at : at + 128], 0.0), axis=0, keepdims=True)
            for at in range(0, column.shape[0], 128)
        ],
        axis=1,
    )


def to_sublanes(line):
    mask = eye()
    return jnp.concatenate(
        [
            jnp.sum(jnp.where(mask, line[:, at : at + 128], 0.0), axis=1, keepdims=True)
            for at in range(0, line.shape[1], 128)
        ],
        axis=0,
    )


TAIL = 16


def pack(mass, lanes):
    high = mass.astype(BF16).astype(F32)
    row = lax.broadcasted_iota(jnp.int32, (TAIL, lanes), 0)
    out = jnp.zeros((TAIL, lanes), F32)
    line = jnp.concatenate([high, mass - high], axis=1)
    for k in range(line.shape[1] // lanes):
        out = jnp.where(row == k, line[:, k * lanes : (k + 1) * lanes], out)
    return out.astype(BF16)


def unpack(tail, count):
    tail = tail.astype(F32)
    line = jnp.concatenate([tail[k : k + 1] for k in range(2 * count // tail.shape[1])], axis=1)
    return line[:, :count] + line[:, count:]


def row_lse_block(logits_ref, rows, colpot, lse_ref):
    step = 32
    columns = []
    for at in range(0, rows.size, step):
        t = logits_ref[pl.ds(rows.start + at, step), :] + colpot
        high = jnp.max(t, axis=1, keepdims=True)
        total = jnp.sum(jnp.exp2(t - high), axis=1, keepdims=True)
        columns.append(high + jnp.log2(total))
    lse_ref[:, rows] = to_lanes(jnp.concatenate(columns, axis=0))


WIDE = 512


def halves_kernel(*refs):
    blocks, outs, sem = refs[:4], refs[4:6], refs[6]
    half = blocks[0].shape[0] // 2
    copies = [
        pltpu.make_async_copy(
            block.at[pl.ds(part * half, half), :], out.at[pl.ds(k * half, half), :], sem.at[part, k]
        )
        for part, out in enumerate(outs)
        for k, block in enumerate(blocks)
    ]
    for copy in copies:
        copy.start()
    for copy in copies:
        copy.wait()


def halves_call(blocks):
    rows, width = blocks[0].shape
    return pl.pallas_call(
        halves_kernel,
        in_specs=[pl.BlockSpec(memory_space=pl.ANY)] * 4,
        out_specs=[pl.BlockSpec(memory_space=pl.ANY)] * 2,
        out_shape=[jax.ShapeDtypeStruct((2 * rows, width), BF16)] * 2,
        scratch_shapes=[pltpu.SemaphoreType.DMA((2, 4))],
        cost_estimate=pl.CostEstimate(
            flops=0, bytes_accessed=16 * rows * width, transcendentals=0
        ),
        compiler_params=pltpu.CompilerParams(vmem_limit_bytes=2 * 2**20),
        name="halves",
    )(*blocks)


def fetch(quarter, spot_ref, lat_refs, buf, sem):
    width = buf.shape[1] // 4
    for n in range(16):
        spot = spot_ref[n]

        @pl.when(spot // 4 == quarter)
        def start():
            lane = pl.multiple_of(lax.rem(spot, 4) * width, width)
            pltpu.make_async_copy(
                lat_refs[n // 2].at[:, pl.ds(n % 2 * width, width)], buf.at[:, pl.ds(lane, width)], sem
            ).start()


def arrive(buf, sem):
    pltpu.make_async_copy(buf, buf, sem).wait()


def near_kernel(spot_ref, *refs):
    line_refs, near_refs, lat_refs = refs[:4], refs[4:8], refs[8:16]
    cross_ref, last_ref, noise_buf, lat_buf, noise_sem, lat_sem, last_sem = refs[16:]
    half = cross_ref.shape[0] // 2
    width = line_refs[0].shape[1]

    def start(quarter):
        slot = lax.rem(quarter, 2)
        fetch(quarter, spot_ref, lat_refs, lat_buf.at[slot], lat_sem.at[slot])
        for k in range(4):
            lanes = pl.ds(k * width, width)

            @pl.when(quarter == 0)
            def whole():
                pltpu.make_async_copy(
                    line_refs[k], noise_buf.at[slot, :, lanes], noise_sem.at[slot]
                ).start()

            for part in range(4):

                @pl.when(quarter == 1 + part // 2)
                def halves():
                    pltpu.make_async_copy(
                        near_refs[part].at[k],
                        noise_buf.at[slot, pl.ds(part % 2 * half, half), lanes],
                        noise_sem.at[slot],
                    ).start()

    start(jnp.int32(0))
    fetch(3, spot_ref, lat_refs, last_ref, last_sem)

    def clear(rows):
        cross_ref[rows, :] = jnp.zeros((128, cross_ref.shape[1]), F32)

    steps_of(cross_ref.shape[0], 128, clear)

    def multiply(quarter, _):
        slot = lax.rem(quarter, 2)
        arrive(noise_buf.at[slot], noise_sem.at[slot])
        arrive(lat_buf.at[slot], lat_sem.at[slot])
        pl.when(quarter < 2)(lambda: start(quarter + 1))
        cross_ref[...] += lax.dot_general(
            noise_buf[slot], lat_buf[slot], (((1,), (1,)), ((), ())), preferred_element_type=F32
        )
        return 0

    lax.fori_loop(0, 3, multiply, 0)
    arrive(last_ref, last_sem)


def in_hbm(value):
    return pltpu.with_memory_space_constraint(value, pltpu.HBM)


def near_call(spots, line, near, lat):
    rows, width = line[0].shape
    cols = lat[0].shape[0]
    return pl.pallas_call(
        near_kernel,
        in_specs=[pl.BlockSpec(memory_space=pltpu.SMEM)] + [pl.BlockSpec(memory_space=pl.ANY)] * 16,
        out_specs=[pl.BlockSpec(memory_space=pltpu.VMEM)] * 2,
        out_shape=[
            jax.ShapeDtypeStruct((rows, cols), F32),
            jax.ShapeDtypeStruct((cols, 4 * width), BF16),
        ],
        scratch_shapes=[
            pltpu.VMEM((2, rows, 4 * width), BF16),
            pltpu.VMEM((2, cols, 4 * width), BF16),
            pltpu.SemaphoreType.DMA((2,)),
            pltpu.SemaphoreType.DMA((2,)),
            pltpu.SemaphoreType.DMA,
        ],
        cost_estimate=pl.CostEstimate(
            flops=8 * rows * cols * 12 * width,
            bytes_accessed=2 * (rows * 12 + cols * 16) * width + 4 * rows * cols,
            transcendentals=0,
        ),
        compiler_params=pltpu.CompilerParams(vmem_limit_bytes=14 * 2**20),
        name="cross_near",
    )(spots, *[in_hbm(v) for v in (*line, *near)], *[v if k % 2 else in_hbm(v) for k, v in enumerate(lat)])


def far_kernel(scale, top_ref, end_ref, lat_ref, cross_ref, logits_ref, lse_ref):
    half = top_ref.shape[1]

    def multiply(lanes):
        for start, part_ref in ((0, top_ref), (half, end_ref)):
            rows = pl.ds(start, half)
            noise = jnp.concatenate([part_ref[k] for k in range(4)], axis=1)
            cross = lax.dot_general(
                noise, lat_ref[lanes, :], (((1,), (1,)), ((), ())), preferred_element_type=F32
            )
            logits_ref[rows, lanes] = (cross_ref[rows, lanes] + cross) * scale

    steps_of(lat_ref.shape[0], WIDE, multiply)
    steps_of(logits_ref.shape[0], 256, lambda rows: row_lse_block(logits_ref, rows, 0.0, lse_ref))


def far_call(far, lat, cross, scale):
    rows, cols = cross.shape
    out_shape = [
        jax.ShapeDtypeStruct((rows, cols), F32),
        jax.ShapeDtypeStruct((1, rows), F32),
    ]
    return in_vmem(
        functools.partial(far_kernel, scale), "cross_far", out_shape,
        2 * rows * cols * lat.shape[1], *far, lat, cross,
    )


def row_kernel(logits_ref, colpot_ref, lse_ref):
    colpot = colpot_ref[...]
    steps_of(logits_ref.shape[0], 256, lambda rows: row_lse_block(logits_ref, rows, colpot, lse_ref))


def row_call(logits, colpot):
    out_shape = [jax.ShapeDtypeStruct((1, logits.shape[0]), F32)]
    return in_vmem(row_kernel, "row_lse", out_shape, 8 * logits.size, logits, colpot)[0]


def col_kernel(logits_ref, rowpot_ref, lse_ref):
    rows, cols = logits_ref.shape
    block = 256

    def some_rows(i, parts):
        first = pl.multiple_of(i * block, block)
        rowpot = to_sublanes(rowpot_ref[:, pl.ds(first, block)])
        rowpot = jnp.broadcast_to(rowpot, (block, 128))
        lines = []
        for at in range(0, cols, 128):
            t = logits_ref[pl.ds(first, block), pl.ds(at, 128)] + rowpot
            high = jnp.max(t, axis=0, keepdims=True)
            total = jnp.sum(jnp.exp2(t - high), axis=0, keepdims=True)
            lines.append(high + jnp.log2(total))
        part = jnp.concatenate(lines, axis=1)
        row = lax.broadcasted_iota(jnp.int32, parts.shape, 0)
        return jnp.where(row == i, part, parts)

    parts = lax.fori_loop(
        0, rows // block, some_rows, jnp.full((rows // block, cols), -jnp.inf, F32)
    )
    high = jnp.max(parts, axis=0, keepdims=True)
    lse_ref[...] = high + jnp.log2(jnp.sum(jnp.exp2(parts - high), axis=0, keepdims=True))


def col_call(logits, rowpot):
    out_shape = [jax.ShapeDtypeStruct((1, logits.shape[1]), F32)]
    return in_vmem(col_kernel, "col_lse", out_shape, 8 * logits.size, logits, rowpot)[0]


def plan_kernel(logits_ref, rowpot_ref, colpot_ref, lat_ref, plan_ref, mass_ref, top_ref, end_ref):
    rows = logits_ref.shape[0]
    half = rows // 2
    colpot = colpot_ref[...]

    def make_half(block):
        sums = []
        for k in range(0, half, 64):
            at = pl.ds(block.start + k, 64)
            if k % 128 == 0:
                rowpot = to_sublanes(rowpot_ref[:, pl.ds(block.start + k, 128)])
            plan = jnp.exp2(logits_ref[at, :] + rowpot[k % 128 : k % 128 + 64] + colpot).astype(BF16)
            plan_ref[at, :] = plan
            sums.append(jnp.sum(plan.astype(F32), axis=1, keepdims=True))
        mass = to_lanes(jnp.concatenate(sums, axis=0))
        mass_ref[:, block] = mass
        share = jnp.dot(plan_ref[block, :], lat_ref[...], preferred_element_type=F32).astype(BF16)
        tail = pack(mass, lat_ref.shape[1])
        for start, out_ref in ((0, top_ref), (half, end_ref)):

            @pl.when(block.start == start)
            def put():
                out_ref[:half, :] = share
                out_ref[half:, :] = tail

    steps_of(rows, half, make_half)


def multiply_into(out_ref, plan_ref, rows, lat_ref, more_ref=None):
    here = pl.ds(0, rows.size)

    def multiply(lanes):
        share = jnp.dot(plan_ref[rows, :], lat_ref[:, lanes], preferred_element_type=F32)
        if more_ref is not None:
            share = share + more_ref[here, lanes].astype(F32)
        out_ref[here, lanes] = share.astype(out_ref.dtype)

    steps_of(lat_ref.shape[1], WIDE, multiply)


def in_vmem(kernel, name, out_shape, flops, *args):
    return pl.pallas_call(
        kernel,
        in_specs=[pl.BlockSpec(memory_space=pltpu.VMEM)] * len(args),
        out_specs=jax.tree.map(lambda _: pl.BlockSpec(memory_space=pltpu.VMEM), out_shape),
        out_shape=out_shape,
        cost_estimate=pl.CostEstimate(
            flops=flops,
            bytes_accessed=sum(a.size * a.dtype.itemsize for a in args),
            transcendentals=0,
        ),
        compiler_params=pltpu.CompilerParams(vmem_limit_bytes=24 * 2**20),
        name=name,
    )(*args)


def plan_call(logits, rowpot, colpot, lat):
    rows, cols = logits.shape
    depth = lat.shape[1]
    share = jax.ShapeDtypeStruct((rows // 2 + TAIL, depth), BF16)
    out_shape = [
        jax.ShapeDtypeStruct((rows, cols), BF16),
        jax.ShapeDtypeStruct((1, rows), F32),
        share,
        share,
    ]
    return in_vmem(
        plan_kernel, "plan", out_shape, 2 * rows * cols * depth, logits, rowpot, colpot, lat
    )


def lat_call(kernel, name, out_shape, flops, spots, lat, scratch, *args):
    space = [pltpu.SMEM] + [pl.ANY] * len(lat) + [pltpu.VMEM] * len(args)
    return pl.pallas_call(
        kernel,
        in_specs=[pl.BlockSpec(memory_space=m) for m in space],
        out_specs=[pl.BlockSpec(memory_space=pltpu.VMEM)] * len(out_shape),
        out_shape=out_shape,
        scratch_shapes=scratch,
        cost_estimate=pl.CostEstimate(
            flops=flops,
            bytes_accessed=sum(a.size * a.dtype.itemsize for a in args),
            transcendentals=0,
        ),
        compiler_params=pltpu.CompilerParams(vmem_limit_bytes=24 * 2**20),
        name=name,
    )(spots, *lat, *args)


def share_kernel(spot_ref, *refs):
    lat_refs, plan_ref, mass_ref = refs[:8], refs[8], refs[9]
    end_ref, top_ref, after_ref, before_ref, sem = refs[10:]
    half = plan_ref.shape[0] // 2
    fetch(1, spot_ref, lat_refs, after_ref, sem.at[0])
    fetch(2, spot_ref, lat_refs, before_ref, sem.at[1])
    for n, (lat_ref, out_ref, rows) in enumerate(
        ((after_ref, end_ref, pl.ds(half, half)), (before_ref, top_ref, pl.ds(0, half)))
    ):
        out_ref[half:, :] = pack(mass_ref[:, rows], out_ref.shape[1])
        arrive(lat_ref, sem.at[n])
        multiply_into(out_ref, plan_ref, rows, lat_ref)


def share_call(spots, lat, plan, mass):
    rows, cols = plan.shape
    depth = 2 * lat[0].shape[1]
    share = jax.ShapeDtypeStruct((rows // 2 + TAIL, depth), BF16)
    quarter = jax.ShapeDtypeStruct((cols, depth), BF16)
    return lat_call(
        share_kernel, "share", [share, share, quarter, quarter], 2 * rows * cols * depth,
        spots, lat, [pltpu.SemaphoreType.DMA((2,))], plan, mass,
    )


def onward_kernel(plan_ref, after_ref, before_ref, mass_ref, top_more, end_more, top_ref, end_ref):
    half = plan_ref.shape[0] // 2
    for lat_ref, more, rows, out_ref in (
        (after_ref, top_more, pl.ds(0, half), top_ref),
        (before_ref, end_more, pl.ds(half, half), end_ref),
    ):
        multiply_into(out_ref, plan_ref, rows, lat_ref, more)
        out_ref[half:, :] = pack(mass_ref[:, rows] + unpack(more[half:, :], half), out_ref.shape[1])


def onward_call(plan, after, before, mass, top_more, end_more):
    rows, cols = plan.shape
    depth = after.shape[1]
    out_shape = [jax.ShapeDtypeStruct((rows // 2 + TAIL, depth), BF16)] * 2
    return in_vmem(
        onward_kernel, "onward", out_shape, 2 * rows * cols * depth,
        plan, after, before, mass, top_more, end_more,
    )


def sum_kernel(own_ref, mass_ref, top_ref, end_ref, keep_ref, total_ref, *part_refs):
    rows = own_ref.shape[0]
    half, width = rows // 2, keep_ref.shape[1]
    for start, more in ((0, top_ref), (half, end_ref)):
        there = pl.ds(start, half)
        total_ref[:, there] = mass_ref[:, there] + unpack(more[half:, :], half)
    tail = pack(total_ref[...], width)
    for start, more in ((0, top_ref), (half, end_ref)):

        def add(here):
            there = pl.ds(start + here.start, here.size)
            for k, out_ref in zip((3, 2, 1, 0), (*part_refs, keep_ref)):
                lanes = pl.ds(k * width, width)
                value = own_ref[there, lanes] + more[here, lanes].astype(F32)
                out_ref[there, :] = value.astype(out_ref.dtype)

        steps_of(half, 128, add)
    for out_ref in part_refs:
        out_ref[rows:, :] = tail


def sum_call(own, mass, *received):
    rows, depth = own.shape
    width = depth // 4
    part = jax.ShapeDtypeStruct((rows + TAIL, width), BF16)
    out_shape = [
        jax.ShapeDtypeStruct((rows, width), F32),
        jax.ShapeDtypeStruct((1, rows), F32),
        part, part, part,
    ]
    return in_vmem(sum_kernel, "sum_s", out_shape, 2 * rows * depth, own, mass, *received)


def finish_kernel(keep_ref, total_ref, *refs):
    part_refs, out_ref, mass_ref = refs[:-2], refs[-2], refs[-1]
    mass = total_ref[...]
    for part in part_refs:
        mass = mass + unpack(part[keep_ref.shape[0] :, :], keep_ref.shape[0])
    mass_ref[...] = mass

    def divide(rows):
        value = keep_ref[rows, :]
        for part in part_refs:
            value = value + part[rows, :].astype(F32)
        out_ref[rows, :] = value / to_sublanes(mass_ref[:, rows])

    steps_of(keep_ref.shape[0], 128, divide)


def finish_call(keep, mass, parts):
    out_shape = [jax.ShapeDtypeStruct(keep.shape, F32), jax.ShapeDtypeStruct(mass.shape, F32)]
    return in_vmem(finish_kernel, "finish", out_shape, 4 * keep.size, keep, mass, *parts)[0]


def own_kernel(spot_ref, *refs):
    lat_refs, (plan_ref, mass_ref, top_ref, end_ref) = refs[:8], refs[8:12]
    out_ref, total_ref, lat_buf, sem = refs[12:]
    half = plan_ref.shape[0] // 2
    fetch(0, spot_ref, lat_refs, lat_buf, sem)
    arrive(lat_buf, sem)
    for rows, more in ((pl.ds(0, half), top_ref), (pl.ds(half, half), end_ref)):
        multiply_into(out_ref.at[rows, :], plan_ref, rows, lat_buf, more)
        total_ref[:, rows] = mass_ref[:, rows] + unpack(more[half:, :], half)


def own_call(spots, lat, plan, mass, top, end):
    rows, cols = plan.shape
    depth = 2 * lat[0].shape[1]
    return lat_call(
        own_kernel,
        "own",
        [jax.ShapeDtypeStruct((rows, depth), F32), jax.ShapeDtypeStruct((1, rows), F32)],
        2 * rows * cols * depth,
        spots, lat, [pltpu.VMEM((cols, depth), BF16), pltpu.SemaphoreType.DMA],
        plan, mass, top, end,
    )


def on_device(noise, latents):
    width = latents.shape[1] * lax.axis_size("row")
    noise_count = noise.shape[0] * lax.axis_size("row")
    latent_count = latents.shape[0] * lax.axis_size("col")
    line, near, far, pieces = gather(noise, latents)
    spots = latent_spots()
    cross, last = near_call(spots, line, near, pieces)
    logits, lse = far_call(far, last, cross, 2.0 / (width * EPSILON) * LOG2E)
    for step in range(ITERS):
        if step:
            lse = row_call(logits, colpot)
        rowpot = -math.log2(noise_count) - over_col(lse, logadd)
        colpot = -math.log2(latent_count) - over_row(col_call(logits, rowpot), logadd)
    plan, mass, far_top, far_end = plan_call(logits, rowpot, colpot, last)
    transported, rowpot, colpot = scatter_sum(
        plan, spots, pieces, far_top, far_end, mass, rowpot, colpot
    )
    return (transported, rowpot.reshape(-1), colpot.reshape(-1))


def solution(mesh):
    in_specs = (P("row", "col"), P("col", "row"))
    out_specs = (P("row", "col"), P("row"), P("col"))
    return jax.shard_map(
        on_device, mesh=mesh, in_specs=in_specs, out_specs=out_specs, check_vma=False
    )
```

```python
import functools
import math

import jax
import jax.numpy as jnp
from jax import lax
from jax.experimental import pallas as pl
from jax.experimental.pallas import tpu as pltpu
from jax.sharding import PartitionSpec as P

ITERS = 3
EPSILON = 0.01
LOG2E = math.log2(math.e)
LN2 = math.log(2.0)
NX, NY, NZ, NC = 4, 4, 4, 2

F32 = jnp.float32
BF16 = jnp.bfloat16


def shift_z(by):
    return [(x * NZ + z, x * NZ + (z + by) % NZ) for x in range(NX) for z in range(NZ)]


def shift_x(by):
    return [(x * NZ + z, (x + by) % NX * NZ + z) for x in range(NX) for z in range(NZ)]


def shift_y(by):
    return [(y * NC + c, (y + by) % NY * NC + c) for y in range(NY) for c in range(NC)]


def swap_core():
    return [(y * NC + c, y * NC + 1 - c) for y in range(NY) for c in range(NC)]


def logadd(parts):
    high = functools.reduce(jnp.maximum, parts)
    total = functools.reduce(jnp.add, [jnp.exp2(p - high) for p in parts])
    return high + jnp.log2(total)


BOTH = ("row", "col")


def spread_y():
    return [
        (y * NC + c, (y + 1 - 2 * c) % NY * NC + c) for y in range(NY) for c in range(NC)
    ]


def everywhere(perms):
    count = NX * NZ
    return [
        (row * count + a, row * count + b) for row in range(NY * NC) for a, b in perms[row % NC]
    ]


def around(value, axis, spread, opposite, combine):
    far = lax.ppermute(value, axis, opposite)
    near = lax.ppermute(value, axis, spread)
    return combine([value, far, near, lax.ppermute(near, "row", swap_core())])


def over_col(value, combine):
    mine = lax.axis_index("row") % NC == 0
    other = lax.ppermute(value, "row", swap_core())
    both = jnp.concatenate(
        [jnp.where(mine, value, other), jnp.where(mine, other, value)], axis=0
    )
    for shift in (shift_z, shift_x):
        both = around(both, BOTH, everywhere([shift(1), shift(-1)]), everywhere([shift(2)] * 2), combine)
    return jnp.where(mine, both[:1], both[1:])


def over_row(value, combine):
    value = combine([value, lax.ppermute(value, "row", swap_core())])
    return around(value, "row", spread_y(), shift_y(2), combine)


ORDER = (0, 1, 3, 2)


def hop_f(value, by):
    return lax.ppermute(value, BOTH, everywhere([shift_z(by), shift_x(by)]))


def hop_s(value, by):
    return lax.ppermute(value, BOTH, everywhere([shift_x(by), shift_z(by)]))


def gather(noise, latents):
    rows, width = noise.shape
    half = rows // 2
    swap = lambda v: lax.ppermute(v, "row", swap_core())
    opposite = hop_f(noise, 2)
    after, before, opposite, other = lax.optimization_barrier(
        (hop_f(noise, -1), hop_f(noise, 1), opposite, swap(latents))
    )
    line = [noise, after, before, opposite]
    near = lax.ppermute(latents, "row", spread_y())
    away = lax.ppermute(latents, "row", [(b, a) for a, b in spread_y()])
    top, end = halves_call(line)
    ready, _, _ = lax.optimization_barrier((near, top, end))
    far = lax.ppermute(ready, "row", spread_y())
    top_m, end_p = hop_s(top, 1), hop_s(end, -1)
    end_m, top_p = hop_s(end, 1), hop_s(top, -1)
    top_far, end_far = hop_s(top_m, 1), hop_s(end_p, -1)
    near_other, away_other, far_other = map(swap, lax.optimization_barrier((near, away, far)))
    split = lambda v: v.reshape(4, half, width)
    lat = [latents, other, near, near_other, away, away_other, far, far_other]
    return (
        line,
        [split(v) for v in (top_p, end_p, top_m, end_m)],
        [split(top_far), split(end_far)],
        lat,
    )


def latent_spots():
    row, col = lax.axis_index("row"), lax.axis_index("col")
    y, core = row // NC, row % NC
    block = lambda dy, flip: (y + dy) % NY * NC + (core if not flip else 1 - core)
    back = jnp.where(core == 0, 3, 1)
    rows = [
        block(0, False), block(0, True), block(back, False), block(4 - back, True),
        block(4 - back, False), block(back, True), block(2, False), block(2, True),
    ]
    at = (jnp.stack(rows)[:, None] * 2 + jnp.arange(2)[None, :]).reshape(-1)
    dx, dz = (at // NZ - col // NZ) % NX, (at % NZ - col % NZ) % NZ
    df, ds = jnp.where(core == 0, dz, dx), jnp.where(core == 0, dx, dz)
    rank = lambda d: jnp.where(d < 2, d, 5 - d)
    return (rank(ds) * 4 + rank(df)).astype(jnp.int32)


def scatter_sum(plan, spots, lat, far_top, far_end, mass, rowpot, colpot):
    barrier = lax.optimization_barrier
    far_top, far_end = hop_s(far_top, 1), hop_s(far_end, -1)
    end, top, after, before = share_call(spots, lat, plan, mass)
    end_m, top_p = hop_s(end, 1), hop_s(top, -1)
    top, end = onward_call(plan, after, before, mass, far_top, far_end)
    top_m, end_p = hop_s(top, 1), hop_s(end, -1)
    plan, rowpot, colpot, _, _ = barrier((plan, rowpot, colpot, top, end))
    own, mass = own_call(spots, lat, plan, mass, top_p, end_m)
    rowpot, colpot = rowpot * LN2, colpot * LN2
    own, top_m, end_p, rowpot, colpot = barrier((own, top_m, end_p, rowpot, colpot))
    keep, mass, *parts = sum_call(own, mass, top_m, end_p)
    parts = [hop_f(v, ORDER[k]) for v, k in zip(parts, (3, 2, 1))]
    return finish_call(keep, mass, parts), rowpot, colpot


def steps_of(total, step, body):
    def turn(i, _):
        body(pl.ds(pl.multiple_of(i * step, step), step))
        return 0

    lax.fori_loop(0, total // step, turn, 0)


def eye():
    return lax.broadcasted_iota(jnp.int32, (128, 128), 0) == lax.broadcasted_iota(
        jnp.int32, (128, 128), 1
    )


def to_lanes(column):
    mask = eye()
    return jnp.concatenate(
        [
            jnp.sum(jnp.where(mask, column[at : at + 128], 0.0), axis=0, keepdims=True)
            for at in range(0, column.shape[0], 128)
        ],
        axis=1,
    )


def to_sublanes(line):
    mask = eye()
    return jnp.concatenate(
        [
            jnp.sum(jnp.where(mask, line[:, at : at + 128], 0.0), axis=1, keepdims=True)
            for at in range(0, line.shape[1], 128)
        ],
        axis=0,
    )


TAIL = 16


def pack(mass, lanes):
    high = mass.astype(BF16).astype(F32)
    row = lax.broadcasted_iota(jnp.int32, (TAIL, lanes), 0)
    out = jnp.zeros((TAIL, lanes), F32)
    line = jnp.concatenate([high, mass - high], axis=1)
    for k in range(line.shape[1] // lanes):
        out = jnp.where(row == k, line[:, k * lanes : (k + 1) * lanes], out)
    return out.astype(BF16)


def unpack(tail, count):
    tail = tail.astype(F32)
    line = jnp.concatenate([tail[k : k + 1] for k in range(2 * count // tail.shape[1])], axis=1)
    return line[:, :count] + line[:, count:]


def row_lse_block(logits_ref, rows, colpot, lse_ref):
    step = 32
    columns = []
    for at in range(0, rows.size, step):
        t = logits_ref[pl.ds(rows.start + at, step), :] + colpot
        high = jnp.max(t, axis=1, keepdims=True)
        total = jnp.sum(jnp.exp2(t - high), axis=1, keepdims=True)
        columns.append(high + jnp.log2(total))
    lse_ref[:, rows] = to_lanes(jnp.concatenate(columns, axis=0))


WIDE = 512


def halves_kernel(*refs):
    blocks, outs, sem = refs[:4], refs[4:6], refs[6]
    half = blocks[0].shape[0] // 2
    copies = [
        pltpu.make_async_copy(
            block.at[pl.ds(part * half, half), :], out.at[pl.ds(k * half, half), :], sem.at[part, k]
        )
        for part, out in enumerate(outs)
        for k, block in enumerate(blocks)
    ]
    for copy in copies:
        copy.start()
    for copy in copies:
        copy.wait()


def halves_call(blocks):
    rows, width = blocks[0].shape
    return pl.pallas_call(
        halves_kernel,
        in_specs=[pl.BlockSpec(memory_space=pl.ANY)] * 4,
        out_specs=[pl.BlockSpec(memory_space=pl.ANY)] * 2,
        out_shape=[jax.ShapeDtypeStruct((2 * rows, width), BF16)] * 2,
        scratch_shapes=[pltpu.SemaphoreType.DMA((2, 4))],
        cost_estimate=pl.CostEstimate(
            flops=0, bytes_accessed=16 * rows * width, transcendentals=0
        ),
        compiler_params=pltpu.CompilerParams(vmem_limit_bytes=2 * 2**20),
        name="halves",
    )(*blocks)


def fetch(quarter, spot_ref, lat_refs, buf, sem):
    width = buf.shape[1] // 4
    for n in range(16):
        spot = spot_ref[n]

        @pl.when(spot // 4 == quarter)
        def start():
            lane = pl.multiple_of(lax.rem(spot, 4) * width, width)
            pltpu.make_async_copy(
                lat_refs[n // 2].at[:, pl.ds(n % 2 * width, width)], buf.at[:, pl.ds(lane, width)], sem
            ).start()


def arrive(buf, sem):
    pltpu.make_async_copy(buf, buf, sem).wait()


def near_kernel(spot_ref, *refs):
    line_refs, near_refs, lat_refs = refs[:4], refs[4:8], refs[8:16]
    cross_ref, last_ref, noise_buf, lat_buf, noise_sem, lat_sem, last_sem = refs[16:]
    half = cross_ref.shape[0] // 2
    width = line_refs[0].shape[1]

    def start(quarter):
        slot = lax.rem(quarter, 2)
        fetch(quarter, spot_ref, lat_refs, lat_buf.at[slot], lat_sem.at[slot])
        for k in range(4):
            lanes = pl.ds(k * width, width)

            @pl.when(quarter == 0)
            def whole():
                pltpu.make_async_copy(
                    line_refs[k], noise_buf.at[slot, :, lanes], noise_sem.at[slot]
                ).start()

            for part in range(4):

                @pl.when(quarter == 1 + part // 2)
                def halves():
                    pltpu.make_async_copy(
                        near_refs[part].at[k],
                        noise_buf.at[slot, pl.ds(part % 2 * half, half), lanes],
                        noise_sem.at[slot],
                    ).start()

    start(jnp.int32(0))
    fetch(3, spot_ref, lat_refs, last_ref, last_sem)

    def clear(rows):
        cross_ref[rows, :] = jnp.zeros((128, cross_ref.shape[1]), F32)

    steps_of(cross_ref.shape[0], 128, clear)

    def multiply(quarter, _):
        slot = lax.rem(quarter, 2)
        arrive(noise_buf.at[slot], noise_sem.at[slot])
        arrive(lat_buf.at[slot], lat_sem.at[slot])
        pl.when(quarter < 2)(lambda: start(quarter + 1))
        cross_ref[...] += lax.dot_general(
            noise_buf[slot], lat_buf[slot], (((1,), (1,)), ((), ())), preferred_element_type=F32
        )
        return 0

    lax.fori_loop(0, 3, multiply, 0)
    arrive(last_ref, last_sem)


def in_hbm(value):
    return pltpu.with_memory_space_constraint(value, pltpu.HBM)


def near_call(spots, line, near, lat):
    rows, width = line[0].shape
    cols = lat[0].shape[0]
    return pl.pallas_call(
        near_kernel,
        in_specs=[pl.BlockSpec(memory_space=pltpu.SMEM)] + [pl.BlockSpec(memory_space=pl.ANY)] * 16,
        out_specs=[pl.BlockSpec(memory_space=pltpu.VMEM)] * 2,
        out_shape=[
            jax.ShapeDtypeStruct((rows, cols), F32),
            jax.ShapeDtypeStruct((cols, 4 * width), BF16),
        ],
        scratch_shapes=[
            pltpu.VMEM((2, rows, 4 * width), BF16),
            pltpu.VMEM((2, cols, 4 * width), BF16),
            pltpu.SemaphoreType.DMA((2,)),
            pltpu.SemaphoreType.DMA((2,)),
            pltpu.SemaphoreType.DMA,
        ],
        cost_estimate=pl.CostEstimate(
            flops=8 * rows * cols * 12 * width,
            bytes_accessed=2 * (rows * 12 + cols * 16) * width + 4 * rows * cols,
            transcendentals=0,
        ),
        compiler_params=pltpu.CompilerParams(vmem_limit_bytes=14 * 2**20),
        name="cross_near",
    )(spots, *[in_hbm(v) for v in (*line, *near)], *[v if k % 2 else in_hbm(v) for k, v in enumerate(lat)])


def far_kernel(scale, top_ref, end_ref, lat_ref, cross_ref, logits_ref, lse_ref):
    half = top_ref.shape[1]

    for start, part_ref in ((0, top_ref), (half, end_ref)):
        rows = pl.ds(start, half)
        noise = jnp.concatenate([part_ref[k] for k in range(4)], axis=1)
        cross = lax.dot_general(
            noise, lat_ref[...], (((1,), (1,)), ((), ())), preferred_element_type=F32
        )
        logits_ref[rows, :] = (cross_ref[rows, :] + cross) * scale
    steps_of(logits_ref.shape[0], 256, lambda rows: row_lse_block(logits_ref, rows, 0.0, lse_ref))


def far_call(far, lat, cross, scale):
    rows, cols = cross.shape
    out_shape = [
        jax.ShapeDtypeStruct((rows, cols), F32),
        jax.ShapeDtypeStruct((1, rows), F32),
    ]
    return in_vmem(
        functools.partial(far_kernel, scale), "cross_far", out_shape,
        2 * rows * cols * lat.shape[1], *far, lat, cross,
    )


def row_kernel(logits_ref, colpot_ref, lse_ref):
    colpot = colpot_ref[...]
    steps_of(logits_ref.shape[0], 256, lambda rows: row_lse_block(logits_ref, rows, colpot, lse_ref))


def row_call(logits, colpot):
    out_shape = [jax.ShapeDtypeStruct((1, logits.shape[0]), F32)]
    return in_vmem(row_kernel, "row_lse", out_shape, 8 * logits.size, logits, colpot)[0]


def col_kernel(logits_ref, rowpot_ref, lse_ref):
    rows, cols = logits_ref.shape
    block = 256

    def some_rows(i, parts):
        first = pl.multiple_of(i * block, block)
        rowpot = to_sublanes(rowpot_ref[:, pl.ds(first, block)])
        rowpot = jnp.broadcast_to(rowpot, (block, 128))
        lines = []
        for at in range(0, cols, 128):
            t = logits_ref[pl.ds(first, block), pl.ds(at, 128)] + rowpot
            high = jnp.max(t, axis=0, keepdims=True)
            total = jnp.sum(jnp.exp2(t - high), axis=0, keepdims=True)
            lines.append(high + jnp.log2(total))
        part = jnp.concatenate(lines, axis=1)
        row = lax.broadcasted_iota(jnp.int32, parts.shape, 0)
        return jnp.where(row == i, part, parts)

    parts = lax.fori_loop(
        0, rows // block, some_rows, jnp.full((rows // block, cols), -jnp.inf, F32)
    )
    high = jnp.max(parts, axis=0, keepdims=True)
    lse_ref[...] = high + jnp.log2(jnp.sum(jnp.exp2(parts - high), axis=0, keepdims=True))


def col_call(logits, rowpot):
    out_shape = [jax.ShapeDtypeStruct((1, logits.shape[1]), F32)]
    return in_vmem(col_kernel, "col_lse", out_shape, 8 * logits.size, logits, rowpot)[0]


def plan_kernel(logits_ref, rowpot_ref, colpot_ref, lat_ref, plan_ref, mass_ref, top_ref, end_ref):
    rows = logits_ref.shape[0]
    half = rows // 2
    colpot = colpot_ref[...]

    def make_half(block):
        sums = []
        for k in range(0, half, 64):
            at = pl.ds(block.start + k, 64)
            if k % 128 == 0:
                rowpot = to_sublanes(rowpot_ref[:, pl.ds(block.start + k, 128)])
            plan = jnp.exp2(logits_ref[at, :] + rowpot[k % 128 : k % 128 + 64] + colpot).astype(BF16)
            plan_ref[at, :] = plan
            sums.append(jnp.sum(plan.astype(F32), axis=1, keepdims=True))
        mass = to_lanes(jnp.concatenate(sums, axis=0))
        mass_ref[:, block] = mass
        share = jnp.dot(plan_ref[block, :], lat_ref[...], preferred_element_type=F32).astype(BF16)
        tail = pack(mass, lat_ref.shape[1])
        for start, out_ref in ((0, top_ref), (half, end_ref)):

            @pl.when(block.start == start)
            def put():
                out_ref[:half, :] = share
                out_ref[half:, :] = tail

    steps_of(rows, half, make_half)


def multiply_into(out_ref, plan_ref, rows, lat_ref, more_ref=None):
    here = pl.ds(0, rows.size)

    def multiply(lanes):
        share = jnp.dot(plan_ref[rows, :], lat_ref[:, lanes], preferred_element_type=F32)
        if more_ref is not None:
            share = share + more_ref[here, lanes].astype(F32)
        out_ref[here, lanes] = share.astype(out_ref.dtype)

    steps_of(lat_ref.shape[1], WIDE, multiply)


def in_vmem(kernel, name, out_shape, flops, *args):
    return pl.pallas_call(
        kernel,
        in_specs=[pl.BlockSpec(memory_space=pltpu.VMEM)] * len(args),
        out_specs=jax.tree.map(lambda _: pl.BlockSpec(memory_space=pltpu.VMEM), out_shape),
        out_shape=out_shape,
        cost_estimate=pl.CostEstimate(
            flops=flops,
            bytes_accessed=sum(a.size * a.dtype.itemsize for a in args),
            transcendentals=0,
        ),
        compiler_params=pltpu.CompilerParams(vmem_limit_bytes=24 * 2**20),
        name=name,
    )(*args)


def plan_call(logits, rowpot, colpot, lat):
    rows, cols = logits.shape
    depth = lat.shape[1]
    share = jax.ShapeDtypeStruct((rows // 2 + TAIL, depth), BF16)
    out_shape = [
        jax.ShapeDtypeStruct((rows, cols), BF16),
        jax.ShapeDtypeStruct((1, rows), F32),
        share,
        share,
    ]
    return in_vmem(
        plan_kernel, "plan", out_shape, 2 * rows * cols * depth, logits, rowpot, colpot, lat
    )


def lat_call(kernel, name, out_shape, flops, spots, lat, scratch, *args):
    space = [pltpu.SMEM] + [pl.ANY] * len(lat) + [pltpu.VMEM] * len(args)
    return pl.pallas_call(
        kernel,
        in_specs=[pl.BlockSpec(memory_space=m) for m in space],
        out_specs=[pl.BlockSpec(memory_space=pltpu.VMEM)] * len(out_shape),
        out_shape=out_shape,
        scratch_shapes=scratch,
        cost_estimate=pl.CostEstimate(
            flops=flops,
            bytes_accessed=sum(a.size * a.dtype.itemsize for a in args),
            transcendentals=0,
        ),
        compiler_params=pltpu.CompilerParams(vmem_limit_bytes=24 * 2**20),
        name=name,
    )(spots, *lat, *args)


def share_kernel(spot_ref, *refs):
    lat_refs, plan_ref, mass_ref = refs[:8], refs[8], refs[9]
    end_ref, top_ref, after_ref, before_ref, sem = refs[10:]
    half = plan_ref.shape[0] // 2
    fetch(1, spot_ref, lat_refs, after_ref, sem.at[0])
    fetch(2, spot_ref, lat_refs, before_ref, sem.at[1])
    for n, (lat_ref, out_ref, rows) in enumerate(
        ((after_ref, end_ref, pl.ds(half, half)), (before_ref, top_ref, pl.ds(0, half)))
    ):
        out_ref[half:, :] = pack(mass_ref[:, rows], out_ref.shape[1])
        arrive(lat_ref, sem.at[n])
        multiply_into(out_ref, plan_ref, rows, lat_ref)


def share_call(spots, lat, plan, mass):
    rows, cols = plan.shape
    depth = 2 * lat[0].shape[1]
    share = jax.ShapeDtypeStruct((rows // 2 + TAIL, depth), BF16)
    quarter = jax.ShapeDtypeStruct((cols, depth), BF16)
    return lat_call(
        share_kernel, "share", [share, share, quarter, quarter], 2 * rows * cols * depth,
        spots, lat, [pltpu.SemaphoreType.DMA((2,))], plan, mass,
    )


def onward_kernel(plan_ref, after_ref, before_ref, mass_ref, top_more, end_more, top_ref, end_ref):
    half = plan_ref.shape[0] // 2
    for lat_ref, more, rows, out_ref in (
        (after_ref, top_more, pl.ds(0, half), top_ref),
        (before_ref, end_more, pl.ds(half, half), end_ref),
    ):
        multiply_into(out_ref, plan_ref, rows, lat_ref, more)
        out_ref[half:, :] = pack(mass_ref[:, rows] + unpack(more[half:, :], half), out_ref.shape[1])


def onward_call(plan, after, before, mass, top_more, end_more):
    rows, cols = plan.shape
    depth = after.shape[1]
    out_shape = [jax.ShapeDtypeStruct((rows // 2 + TAIL, depth), BF16)] * 2
    return in_vmem(
        onward_kernel, "onward", out_shape, 2 * rows * cols * depth,
        plan, after, before, mass, top_more, end_more,
    )


def sum_kernel(own_ref, mass_ref, top_ref, end_ref, keep_ref, total_ref, *part_refs):
    rows = own_ref.shape[0]
    half, width = rows // 2, keep_ref.shape[1]
    for start, more in ((0, top_ref), (half, end_ref)):
        there = pl.ds(start, half)
        total_ref[:, there] = mass_ref[:, there] + unpack(more[half:, :], half)
    tail = pack(total_ref[...], width)
    for start, more in ((0, top_ref), (half, end_ref)):

        def add(here):
            there = pl.ds(start + here.start, here.size)
            for k, out_ref in zip((3, 2, 1, 0), (*part_refs, keep_ref)):
                lanes = pl.ds(k * width, width)
                value = own_ref[there, lanes] + more[here, lanes].astype(F32)
                out_ref[there, :] = value.astype(out_ref.dtype)

        steps_of(half, 128, add)
    for out_ref in part_refs:
        out_ref[rows:, :] = tail


def sum_call(own, mass, *received):
    rows, depth = own.shape
    width = depth // 4
    part = jax.ShapeDtypeStruct((rows + TAIL, width), BF16)
    out_shape = [
        jax.ShapeDtypeStruct((rows, width), F32),
        jax.ShapeDtypeStruct((1, rows), F32),
        part, part, part,
    ]
    return in_vmem(sum_kernel, "sum_s", out_shape, 2 * rows * depth, own, mass, *received)


def finish_kernel(keep_ref, total_ref, *refs):
    part_refs, out_ref = refs[:-1], refs[-1]
    rows = keep_ref.shape[0]
    mass = total_ref[...]
    for part in part_refs:
        mass = mass + unpack(part[rows:, :], rows)
    step = 128
    for at in range(0, rows, step):
        there = pl.ds(at, step)
        value = keep_ref[there, :]
        for part in part_refs:
            value = value + part[there, :].astype(F32)
        out_ref[there, :] = (value / to_sublanes(mass[:, at : at + step])).astype(BF16)


def finish_call(keep, mass, parts):
    out_shape = [jax.ShapeDtypeStruct(keep.shape, BF16)]
    return in_vmem(finish_kernel, "finish", out_shape, 4 * keep.size, keep, mass, *parts)[0]


def own_kernel(spot_ref, *refs):
    lat_refs, (plan_ref, mass_ref, top_ref, end_ref) = refs[:8], refs[8:12]
    out_ref, total_ref, lat_buf, sem = refs[12:]
    half = plan_ref.shape[0] // 2
    fetch(0, spot_ref, lat_refs, lat_buf, sem)
    arrive(lat_buf, sem)
    for rows, more in ((pl.ds(0, half), top_ref), (pl.ds(half, half), end_ref)):
        multiply_into(out_ref.at[rows, :], plan_ref, rows, lat_buf, more)
        total_ref[:, rows] = mass_ref[:, rows] + unpack(more[half:, :], half)


def own_call(spots, lat, plan, mass, top, end):
    rows, cols = plan.shape
    depth = 2 * lat[0].shape[1]
    return lat_call(
        own_kernel,
        "own",
        [jax.ShapeDtypeStruct((rows, depth), F32), jax.ShapeDtypeStruct((1, rows), F32)],
        2 * rows * cols * depth,
        spots, lat, [pltpu.VMEM((cols, depth), BF16), pltpu.SemaphoreType.DMA],
        plan, mass, top, end,
    )


def on_device(noise, latents):
    width = latents.shape[1] * lax.axis_size("row")
    noise_count = noise.shape[0] * lax.axis_size("row")
    latent_count = latents.shape[0] * lax.axis_size("col")
    line, near, far, pieces = gather(noise, latents)
    spots = latent_spots()
    cross, last = near_call(spots, line, near, pieces)
    logits, lse = far_call(far, last, cross, 2.0 / (width * EPSILON) * LOG2E)
    for step in range(ITERS):
        if step:
            lse = row_call(logits, colpot)
        rowpot = -math.log2(noise_count) - over_col(lse, logadd)
        colpot = -math.log2(latent_count) - over_row(col_call(logits, rowpot), logadd)
    plan, mass, far_top, far_end = plan_call(logits, rowpot, colpot, last)
    transported, rowpot, colpot = scatter_sum(
        plan, spots, pieces, far_top, far_end, mass, rowpot, colpot
    )
    return (transported, rowpot.reshape(-1), colpot.reshape(-1))


def solution(mesh):
    in_specs = (P("row", "col"), P("col", "row"))
    out_specs = (P("row", "col"), P("row"), P("col"))
    return jax.shard_map(
        on_device, mesh=mesh, in_specs=in_specs, out_specs=out_specs, check_vma=False
    )
```

```python
import functools
import math

import jax
import jax.numpy as jnp
from jax import lax
from jax.experimental import pallas as pl
from jax.experimental.pallas import tpu as pltpu
from jax.sharding import PartitionSpec as P

ITERS = 3
EPSILON = 0.01
LOG2E = math.log2(math.e)
LN2 = math.log(2.0)
NX, NY, NZ, NC = 4, 4, 4, 2

F32 = jnp.float32
BF16 = jnp.bfloat16


def shift_z(by):
    return [(x * NZ + z, x * NZ + (z + by) % NZ) for x in range(NX) for z in range(NZ)]


def shift_x(by):
    return [(x * NZ + z, (x + by) % NX * NZ + z) for x in range(NX) for z in range(NZ)]


def shift_y(by):
    return [(y * NC + c, (y + by) % NY * NC + c) for y in range(NY) for c in range(NC)]


def swap_core():
    return [(y * NC + c, y * NC + 1 - c) for y in range(NY) for c in range(NC)]


def logadd(parts):
    high = functools.reduce(jnp.maximum, parts)
    total = functools.reduce(jnp.add, [jnp.exp2(p - high) for p in parts])
    return high + jnp.log2(total)


BOTH = ("row", "col")


def spread_y():
    return [
        (y * NC + c, (y + 1 - 2 * c) % NY * NC + c) for y in range(NY) for c in range(NC)
    ]


def everywhere(perms):
    count = NX * NZ
    return [
        (row * count + a, row * count + b) for row in range(NY * NC) for a, b in perms[row % NC]
    ]


def around(value, axis, spread, opposite, combine):
    far = lax.ppermute(value, axis, opposite)
    near = lax.ppermute(value, axis, spread)
    return combine([value, far, near, lax.ppermute(near, "row", swap_core())])


def over_col(value, combine):
    mine = lax.axis_index("row") % NC == 0
    other = lax.ppermute(value, "row", swap_core())
    both = jnp.concatenate(
        [jnp.where(mine, value, other), jnp.where(mine, other, value)], axis=0
    )
    for shift in (shift_z, shift_x):
        both = around(both, BOTH, everywhere([shift(1), shift(-1)]), everywhere([shift(2)] * 2), combine)
    return jnp.where(mine, both[:1], both[1:])


def over_row(value, combine):
    value = combine([value, lax.ppermute(value, "row", swap_core())])
    return around(value, "row", spread_y(), shift_y(2), combine)


ORDER = (0, 1, 3, 2)


def hop_f(value, by):
    return lax.ppermute(value, BOTH, everywhere([shift_z(by), shift_x(by)]))


def hop_s(value, by):
    return lax.ppermute(value, BOTH, everywhere([shift_x(by), shift_z(by)]))


def gather(noise, latents):
    rows, width = noise.shape
    half = rows // 2
    swap = lambda v: lax.ppermute(v, "row", swap_core())
    opposite = hop_f(noise, 2)
    after, before, opposite, other = lax.optimization_barrier(
        (hop_f(noise, -1), hop_f(noise, 1), opposite, swap(latents))
    )
    line = [noise, after, before, opposite]
    near = lax.ppermute(latents, "row", spread_y())
    away = lax.ppermute(latents, "row", [(b, a) for a, b in spread_y()])
    top, end = halves_call(line)
    ready, _, _ = lax.optimization_barrier((near, top, end))
    far = lax.ppermute(ready, "row", spread_y())
    top_m, end_p = hop_s(top, 1), hop_s(end, -1)
    end_m, top_p = hop_s(end, 1), hop_s(top, -1)
    top_far, end_far = hop_s(top_m, 1), hop_s(end_p, -1)
    near_other, away_other, far_other = map(swap, lax.optimization_barrier((near, away, far)))
    split = lambda v: v.reshape(4, half, width)
    lat = [latents, other, near, near_other, away, away_other, far, far_other]
    return (
        line,
        [split(v) for v in (top_p, end_p, top_m, end_m)],
        [split(top_far), split(end_far)],
        lat,
    )


def latent_spots():
    row, col = lax.axis_index("row"), lax.axis_index("col")
    y, core = row // NC, row % NC
    block = lambda dy, flip: (y + dy) % NY * NC + (core if not flip else 1 - core)
    back = jnp.where(core == 0, 3, 1)
    rows = [
        block(0, False), block(0, True), block(back, False), block(4 - back, True),
        block(4 - back, False), block(back, True), block(2, False), block(2, True),
    ]
    at = (jnp.stack(rows)[:, None] * 2 + jnp.arange(2)[None, :]).reshape(-1)
    dx, dz = (at // NZ - col // NZ) % NX, (at % NZ - col % NZ) % NZ
    df, ds = jnp.where(core == 0, dz, dx), jnp.where(core == 0, dx, dz)
    rank = lambda d: jnp.where(d < 2, d, 5 - d)
    return (rank(ds) * 4 + rank(df)).astype(jnp.int32)


def scatter_sum(plan, spots, lat, far_top, far_end, mass, rowpot, colpot):
    barrier = lax.optimization_barrier
    far_top, far_end = hop_s(far_top, 1), hop_s(far_end, -1)
    end, top, after, before = share_call(spots, lat, plan, mass)
    end_m, top_p = hop_s(end, 1), hop_s(top, -1)
    top, end = onward_call(plan, after, before, mass, far_top, far_end)
    top_m, end_p = hop_s(top, 1), hop_s(end, -1)
    plan, rowpot, colpot, _, _ = barrier((plan, rowpot, colpot, top, end))
    own, mass = own_call(spots, lat, plan, mass, top_p, end_m)
    rowpot, colpot = rowpot * LN2, colpot * LN2
    own, top_m, end_p, rowpot, colpot = barrier((own, top_m, end_p, rowpot, colpot))
    keep, mass, *parts = sum_call(own, mass, top_m, end_p)
    parts = [hop_f(v, ORDER[k]) for v, k in zip(parts, (3, 2, 1))]
    return finish_call(keep, mass, parts), rowpot, colpot


def steps_of(total, step, body):
    def turn(i, _):
        body(pl.ds(pl.multiple_of(i * step, step), step))
        return 0

    lax.fori_loop(0, total // step, turn, 0)


def eye():
    return lax.broadcasted_iota(jnp.int32, (128, 128), 0) == lax.broadcasted_iota(
        jnp.int32, (128, 128), 1
    )


def to_lanes(column):
    mask = eye()
    return jnp.concatenate(
        [
            jnp.sum(jnp.where(mask, column[at : at + 128], 0.0), axis=0, keepdims=True)
            for at in range(0, column.shape[0], 128)
        ],
        axis=1,
    )


def to_sublanes(line):
    mask = eye()
    return jnp.concatenate(
        [
            jnp.sum(jnp.where(mask, line[:, at : at + 128], 0.0), axis=1, keepdims=True)
            for at in range(0, line.shape[1], 128)
        ],
        axis=0,
    )


TAIL = 16


def pack(mass, lanes):
    high = mass.astype(BF16).astype(F32)
    row = lax.broadcasted_iota(jnp.int32, (TAIL, lanes), 0)
    out = jnp.zeros((TAIL, lanes), F32)
    line = jnp.concatenate([high, mass - high], axis=1)
    for k in range(line.shape[1] // lanes):
        out = jnp.where(row == k, line[:, k * lanes : (k + 1) * lanes], out)
    return out.astype(BF16)


def unpack(tail, count):
    tail = tail.astype(F32)
    line = jnp.concatenate([tail[k : k + 1] for k in range(2 * count // tail.shape[1])], axis=1)
    return line[:, :count] + line[:, count:]


def row_lse_block(logits_ref, rows, colpot, lse_ref):
    step = 32
    columns = []
    for at in range(0, rows.size, step):
        t = logits_ref[pl.ds(rows.start + at, step), :] + colpot
        high = jnp.max(t, axis=1, keepdims=True)
        total = jnp.sum(jnp.exp2(t - high), axis=1, keepdims=True)
        columns.append(high + jnp.log2(total))
    lse_ref[:, rows] = to_lanes(jnp.concatenate(columns, axis=0))


WIDE = 512


def halves_kernel(*refs):
    blocks, outs, sem = refs[:4], refs[4:6], refs[6]
    half = blocks[0].shape[0] // 2
    copies = [
        pltpu.make_async_copy(
            block.at[pl.ds(part * half, half), :], out.at[pl.ds(k * half, half), :], sem.at[part, k]
        )
        for part, out in enumerate(outs)
        for k, block in enumerate(blocks)
    ]
    for copy in copies:
        copy.start()
    for copy in copies:
        copy.wait()


def halves_call(blocks):
    rows, width = blocks[0].shape
    return pl.pallas_call(
        halves_kernel,
        in_specs=[pl.BlockSpec(memory_space=pl.ANY)] * 4,
        out_specs=[pl.BlockSpec(memory_space=pl.ANY)] * 2,
        out_shape=[jax.ShapeDtypeStruct((2 * rows, width), BF16)] * 2,
        scratch_shapes=[pltpu.SemaphoreType.DMA((2, 4))],
        cost_estimate=pl.CostEstimate(
            flops=0, bytes_accessed=16 * rows * width, transcendentals=0
        ),
        compiler_params=pltpu.CompilerParams(vmem_limit_bytes=2 * 2**20),
        name="halves",
    )(*blocks)


def fetch(quarter, spot_ref, lat_refs, buf, sem):
    width = buf.shape[1] // 4
    for n in range(16):
        spot = spot_ref[n]

        @pl.when(spot // 4 == quarter)
        def start():
            lane = pl.multiple_of(lax.rem(spot, 4) * width, width)
            pltpu.make_async_copy(
                lat_refs[n // 2].at[:, pl.ds(n % 2 * width, width)], buf.at[:, pl.ds(lane, width)], sem
            ).start()


def arrive(buf, sem):
    pltpu.make_async_copy(buf, buf, sem).wait()


def near_kernel(spot_ref, *refs):
    line_refs, near_refs, lat_refs = refs[:4], refs[4:8], refs[8:16]
    cross_ref, last_ref, noise_buf, lat_buf, noise_sem, lat_sem, last_sem = refs[16:]
    half = cross_ref.shape[0] // 2
    width = line_refs[0].shape[1]

    def start(quarter):
        slot = lax.rem(quarter, 2)
        fetch(quarter, spot_ref, lat_refs, lat_buf.at[slot], lat_sem.at[slot])
        for k in range(4):
            lanes = pl.ds(k * width, width)

            @pl.when(quarter == 0)
            def whole():
                pltpu.make_async_copy(
                    line_refs[k], noise_buf.at[slot, :, lanes], noise_sem.at[slot]
                ).start()

            for part in range(4):

                @pl.when(quarter == 1 + part // 2)
                def halves():
                    pltpu.make_async_copy(
                        near_refs[part].at[k],
                        noise_buf.at[slot, pl.ds(part % 2 * half, half), lanes],
                        noise_sem.at[slot],
                    ).start()

    start(jnp.int32(0))
    fetch(3, spot_ref, lat_refs, last_ref, last_sem)

    def clear(rows):
        cross_ref[rows, :] = jnp.zeros((128, cross_ref.shape[1]), F32)

    steps_of(cross_ref.shape[0], 128, clear)

    def multiply(quarter, _):
        slot = lax.rem(quarter, 2)
        arrive(noise_buf.at[slot], noise_sem.at[slot])
        arrive(lat_buf.at[slot], lat_sem.at[slot])
        pl.when(quarter < 2)(lambda: start(quarter + 1))
        cross_ref[...] += lax.dot_general(
            noise_buf[slot], lat_buf[slot], (((1,), (1,)), ((), ())), preferred_element_type=F32
        )
        return 0

    lax.fori_loop(0, 3, multiply, 0)
    arrive(last_ref, last_sem)


def in_hbm(value):
    return pltpu.with_memory_space_constraint(value, pltpu.HBM)


def near_call(spots, line, near, lat):
    rows, width = line[0].shape
    cols = lat[0].shape[0]
    return pl.pallas_call(
        near_kernel,
        in_specs=[pl.BlockSpec(memory_space=pltpu.SMEM)] + [pl.BlockSpec(memory_space=pl.ANY)] * 16,
        out_specs=[pl.BlockSpec(memory_space=pltpu.VMEM)] * 2,
        out_shape=[
            jax.ShapeDtypeStruct((rows, cols), F32),
            jax.ShapeDtypeStruct((cols, 4 * width), BF16),
        ],
        scratch_shapes=[
            pltpu.VMEM((2, rows, 4 * width), BF16),
            pltpu.VMEM((2, cols, 4 * width), BF16),
            pltpu.SemaphoreType.DMA((2,)),
            pltpu.SemaphoreType.DMA((2,)),
            pltpu.SemaphoreType.DMA,
        ],
        cost_estimate=pl.CostEstimate(
            flops=8 * rows * cols * 12 * width,
            bytes_accessed=2 * (rows * 12 + cols * 16) * width + 4 * rows * cols,
            transcendentals=0,
        ),
        compiler_params=pltpu.CompilerParams(vmem_limit_bytes=14 * 2**20),
        name="cross_near",
    )(spots, *[in_hbm(v) for v in (*line, *near)], *[v if k % 2 else in_hbm(v) for k, v in enumerate(lat)])


def far_kernel(scale, top_ref, end_ref, lat_ref, cross_ref, logits_ref, lse_ref):
    half = top_ref.shape[1]

    for start, part_ref in ((0, top_ref), (half, end_ref)):
        rows = pl.ds(start, half)
        noise = jnp.concatenate([part_ref[k] for k in range(4)], axis=1)
        cross = lax.dot_general(
            noise, lat_ref[...], (((1,), (1,)), ((), ())), preferred_element_type=F32
        )
        logits_ref[rows, :] = (cross_ref[rows, :] + cross) * scale
    steps_of(logits_ref.shape[0], 256, lambda rows: row_lse_block(logits_ref, rows, 0.0, lse_ref))


def far_call(far, lat, cross, scale):
    rows, cols = cross.shape
    out_shape = [
        jax.ShapeDtypeStruct((rows, cols), F32),
        jax.ShapeDtypeStruct((1, rows), F32),
    ]
    return in_vmem(
        functools.partial(far_kernel, scale), "cross_far", out_shape,
        2 * rows * cols * lat.shape[1], *far, lat, cross,
    )


def row_kernel(logits_ref, colpot_ref, lse_ref):
    colpot = colpot_ref[...]
    steps_of(logits_ref.shape[0], 256, lambda rows: row_lse_block(logits_ref, rows, colpot, lse_ref))


def row_call(logits, colpot):
    out_shape = [jax.ShapeDtypeStruct((1, logits.shape[0]), F32)]
    return in_vmem(row_kernel, "row_lse", out_shape, 8 * logits.size, logits, colpot)[0]


def col_kernel(logits_ref, rowpot_ref, lse_ref):
    rows, cols = logits_ref.shape
    block = 256

    def some_rows(i, parts):
        first = pl.multiple_of(i * block, block)
        rowpot = to_sublanes(rowpot_ref[:, pl.ds(first, block)])
        rowpot = jnp.broadcast_to(rowpot, (block, 128))
        lines = []
        for at in range(0, cols, 128):
            t = logits_ref[pl.ds(first, block), pl.ds(at, 128)] + rowpot
            high = jnp.max(t, axis=0, keepdims=True)
            total = jnp.sum(jnp.exp2(t - high), axis=0, keepdims=True)
            lines.append(high + jnp.log2(total))
        part = jnp.concatenate(lines, axis=1)
        row = lax.broadcasted_iota(jnp.int32, parts.shape, 0)
        return jnp.where(row == i, part, parts)

    parts = lax.fori_loop(
        0, rows // block, some_rows, jnp.full((rows // block, cols), -jnp.inf, F32)
    )
    high = jnp.max(parts, axis=0, keepdims=True)
    lse_ref[...] = high + jnp.log2(jnp.sum(jnp.exp2(parts - high), axis=0, keepdims=True))


def col_call(logits, rowpot):
    out_shape = [jax.ShapeDtypeStruct((1, logits.shape[1]), F32)]
    return in_vmem(col_kernel, "col_lse", out_shape, 8 * logits.size, logits, rowpot)[0]


def plan_kernel(logits_ref, rowpot_ref, colpot_ref, lat_ref, plan_ref, mass_ref, top_ref, end_ref):
    rows = logits_ref.shape[0]
    half = rows // 2
    colpot = colpot_ref[...]

    def make_half(block):
        sums = []
        for k in range(0, half, 64):
            at = pl.ds(block.start + k, 64)
            if k % 128 == 0:
                rowpot = to_sublanes(rowpot_ref[:, pl.ds(block.start + k, 128)])
            plan = jnp.exp2(logits_ref[at, :] + rowpot[k % 128 : k % 128 + 64] + colpot).astype(BF16)
            plan_ref[at, :] = plan
            sums.append(jnp.sum(plan.astype(F32), axis=1, keepdims=True))
        mass = to_lanes(jnp.concatenate(sums, axis=0))
        mass_ref[:, block] = mass
        share = jnp.dot(plan_ref[block, :], lat_ref[...], preferred_element_type=F32).astype(BF16)
        tail = pack(mass, lat_ref.shape[1])
        for start, out_ref in ((0, top_ref), (half, end_ref)):

            @pl.when(block.start == start)
            def put():
                out_ref[:half, :] = share
                out_ref[half:, :] = tail

    steps_of(rows, half, make_half)


def multiply_into(out_ref, plan_ref, rows, lat_ref, more_ref=None):
    here = pl.ds(0, rows.size)

    def multiply(lanes):
        share = jnp.dot(plan_ref[rows, :], lat_ref[:, lanes], preferred_element_type=F32)
        if more_ref is not None:
            share = share + more_ref[here, lanes].astype(F32)
        out_ref[here, lanes] = share.astype(out_ref.dtype)

    if more_ref is not None and out_ref.dtype == BF16:
        multiply(pl.ds(0, lat_ref.shape[1]))
    else:
        steps_of(lat_ref.shape[1], WIDE, multiply)


def in_vmem(kernel, name, out_shape, flops, *args):
    return pl.pallas_call(
        kernel,
        in_specs=[pl.BlockSpec(memory_space=pltpu.VMEM)] * len(args),
        out_specs=jax.tree.map(lambda _: pl.BlockSpec(memory_space=pltpu.VMEM), out_shape),
        out_shape=out_shape,
        cost_estimate=pl.CostEstimate(
            flops=flops,
            bytes_accessed=sum(a.size * a.dtype.itemsize for a in args),
            transcendentals=0,
        ),
        compiler_params=pltpu.CompilerParams(vmem_limit_bytes=24 * 2**20),
        name=name,
    )(*args)


def plan_call(logits, rowpot, colpot, lat):
    rows, cols = logits.shape
    depth = lat.shape[1]
    share = jax.ShapeDtypeStruct((rows // 2 + TAIL, depth), BF16)
    out_shape = [
        jax.ShapeDtypeStruct((rows, cols), BF16),
        jax.ShapeDtypeStruct((1, rows), F32),
        share,
        share,
    ]
    return in_vmem(
        plan_kernel, "plan", out_shape, 2 * rows * cols * depth, logits, rowpot, colpot, lat
    )


def lat_call(kernel, name, out_shape, flops, spots, lat, scratch, *args):
    space = [pltpu.SMEM] + [pl.ANY] * len(lat) + [pltpu.VMEM] * len(args)
    return pl.pallas_call(
        kernel,
        in_specs=[pl.BlockSpec(memory_space=m) for m in space],
        out_specs=[pl.BlockSpec(memory_space=pltpu.VMEM)] * len(out_shape),
        out_shape=out_shape,
        scratch_shapes=scratch,
        cost_estimate=pl.CostEstimate(
            flops=flops,
            bytes_accessed=sum(a.size * a.dtype.itemsize for a in args),
            transcendentals=0,
        ),
        compiler_params=pltpu.CompilerParams(vmem_limit_bytes=24 * 2**20),
        name=name,
    )(spots, *lat, *args)


def share_kernel(spot_ref, *refs):
    lat_refs, plan_ref, mass_ref = refs[:8], refs[8], refs[9]
    end_ref, top_ref, after_ref, before_ref, sem = refs[10:]
    half = plan_ref.shape[0] // 2
    fetch(1, spot_ref, lat_refs, after_ref, sem.at[0])
    fetch(2, spot_ref, lat_refs, before_ref, sem.at[1])
    for n, (lat_ref, out_ref, rows) in enumerate(
        ((after_ref, end_ref, pl.ds(half, half)), (before_ref, top_ref, pl.ds(0, half)))
    ):
        out_ref[half:, :] = pack(mass_ref[:, rows], out_ref.shape[1])
        arrive(lat_ref, sem.at[n])
        multiply_into(out_ref, plan_ref, rows, lat_ref)


def share_call(spots, lat, plan, mass):
    rows, cols = plan.shape
    depth = 2 * lat[0].shape[1]
    share = jax.ShapeDtypeStruct((rows // 2 + TAIL, depth), BF16)
    quarter = jax.ShapeDtypeStruct((cols, depth), BF16)
    return lat_call(
        share_kernel, "share", [share, share, quarter, quarter], 2 * rows * cols * depth,
        spots, lat, [pltpu.SemaphoreType.DMA((2,))], plan, mass,
    )


def onward_kernel(plan_ref, after_ref, before_ref, mass_ref, top_more, end_more, top_ref, end_ref):
    half = plan_ref.shape[0] // 2
    for lat_ref, more, rows, out_ref in (
        (after_ref, top_more, pl.ds(0, half), top_ref),
        (before_ref, end_more, pl.ds(half, half), end_ref),
    ):
        multiply_into(out_ref, plan_ref, rows, lat_ref, more)
        out_ref[half:, :] = pack(mass_ref[:, rows] + unpack(more[half:, :], half), out_ref.shape[1])


def onward_call(plan, after, before, mass, top_more, end_more):
    rows, cols = plan.shape
    depth = after.shape[1]
    out_shape = [jax.ShapeDtypeStruct((rows // 2 + TAIL, depth), BF16)] * 2
    return in_vmem(
        onward_kernel, "onward", out_shape, 2 * rows * cols * depth,
        plan, after, before, mass, top_more, end_more,
    )


def sum_kernel(own_ref, mass_ref, top_ref, end_ref, keep_ref, total_ref, *part_refs):
    rows = own_ref.shape[0]
    half, width = rows // 2, keep_ref.shape[1]
    for start, more in ((0, top_ref), (half, end_ref)):
        there = pl.ds(start, half)
        total_ref[:, there] = mass_ref[:, there] + unpack(more[half:, :], half)
    tail = pack(total_ref[...], width)
    for start, more in ((0, top_ref), (half, end_ref)):

        def add(here):
            there = pl.ds(start + here.start, here.size)
            for k, out_ref in zip((3, 2, 1, 0), (*part_refs, keep_ref)):
                lanes = pl.ds(k * width, width)
                value = own_ref[there, lanes] + more[here, lanes].astype(F32)
                out_ref[there, :] = value.astype(out_ref.dtype)

        steps_of(half, 128, add)
    for out_ref in part_refs:
        out_ref[rows:, :] = tail


def sum_call(own, mass, *received):
    rows, depth = own.shape
    width = depth // 4
    part = jax.ShapeDtypeStruct((rows + TAIL, width), BF16)
    out_shape = [
        jax.ShapeDtypeStruct((rows, width), F32),
        jax.ShapeDtypeStruct((1, rows), F32),
        part, part, part,
    ]
    return in_vmem(sum_kernel, "sum_s", out_shape, 2 * rows * depth, own, mass, *received)


def finish_kernel(keep_ref, total_ref, *refs):
    part_refs, out_ref = refs[:-1], refs[-1]
    rows = keep_ref.shape[0]
    mass = total_ref[...]
    for part in part_refs:
        mass = mass + unpack(part[rows:, :], rows)
    step = 128
    for at in range(0, rows, step):
        there = pl.ds(at, step)
        value = keep_ref[there, :]
        for part in part_refs:
            value = value + part[there, :].astype(F32)
        out_ref[there, :] = (value / to_sublanes(mass[:, at : at + step])).astype(BF16)


def finish_call(keep, mass, parts):
    out_shape = [jax.ShapeDtypeStruct(keep.shape, BF16)]
    return in_vmem(finish_kernel, "finish", out_shape, 4 * keep.size, keep, mass, *parts)[0]


def own_kernel(spot_ref, *refs):
    lat_refs, (plan_ref, mass_ref, top_ref, end_ref) = refs[:8], refs[8:12]
    out_ref, total_ref, lat_buf, sem = refs[12:]
    half = plan_ref.shape[0] // 2
    fetch(0, spot_ref, lat_refs, lat_buf, sem)
    arrive(lat_buf, sem)
    for rows, more in ((pl.ds(0, half), top_ref), (pl.ds(half, half), end_ref)):
        multiply_into(out_ref.at[rows, :], plan_ref, rows, lat_buf, more)
        total_ref[:, rows] = mass_ref[:, rows] + unpack(more[half:, :], half)


def own_call(spots, lat, plan, mass, top, end):
    rows, cols = plan.shape
    depth = 2 * lat[0].shape[1]
    return lat_call(
        own_kernel,
        "own",
        [jax.ShapeDtypeStruct((rows, depth), F32), jax.ShapeDtypeStruct((1, rows), F32)],
        2 * rows * cols * depth,
        spots, lat, [pltpu.VMEM((cols, depth), BF16), pltpu.SemaphoreType.DMA],
        plan, mass, top, end,
    )


def on_device(noise, latents):
    width = latents.shape[1] * lax.axis_size("row")
    noise_count = noise.shape[0] * lax.axis_size("row")
    latent_count = latents.shape[0] * lax.axis_size("col")
    line, near, far, pieces = gather(noise, latents)
    spots = latent_spots()
    cross, last = near_call(spots, line, near, pieces)
    logits, lse = far_call(far, last, cross, 2.0 / (width * EPSILON) * LOG2E)
    for step in range(ITERS):
        if step:
            lse = row_call(logits, colpot)
        rowpot = -math.log2(noise_count) - over_col(lse, logadd)
        colpot = -math.log2(latent_count) - over_row(col_call(logits, rowpot), logadd)
    plan, mass, far_top, far_end = plan_call(logits, rowpot, colpot, last)
    transported, rowpot, colpot = scatter_sum(
        plan, spots, pieces, far_top, far_end, mass, rowpot, colpot
    )
    return (transported, rowpot.reshape(-1), colpot.reshape(-1))


def solution(mesh):
    in_specs = (P("row", "col"), P("col", "row"))
    out_specs = (P("row", "col"), P("row"), P("col"))
    return jax.shard_map(
        on_device, mesh=mesh, in_specs=in_specs, out_specs=out_specs, check_vma=False
    )
```

```python
import functools
import math

import jax
import jax.numpy as jnp
from jax import lax
from jax.experimental import pallas as pl
from jax.experimental.pallas import tpu as pltpu
from jax.sharding import PartitionSpec as P

ITERS = 3
EPSILON = 0.01
LOG2E = math.log2(math.e)
LN2 = math.log(2.0)
NX, NY, NZ, NC = 4, 4, 4, 2

F32 = jnp.float32
BF16 = jnp.bfloat16


def shift_z(by):
    return [(x * NZ + z, x * NZ + (z + by) % NZ) for x in range(NX) for z in range(NZ)]


def shift_x(by):
    return [(x * NZ + z, (x + by) % NX * NZ + z) for x in range(NX) for z in range(NZ)]


def shift_y(by):
    return [(y * NC + c, (y + by) % NY * NC + c) for y in range(NY) for c in range(NC)]


def swap_core():
    return [(y * NC + c, y * NC + 1 - c) for y in range(NY) for c in range(NC)]


def logadd(parts):
    high = functools.reduce(jnp.maximum, parts)
    total = functools.reduce(jnp.add, [jnp.exp2(p - high) for p in parts])
    return high + jnp.log2(total)


BOTH = ("row", "col")


def spread_y():
    return [
        (y * NC + c, (y + 1 - 2 * c) % NY * NC + c) for y in range(NY) for c in range(NC)
    ]


def everywhere(perms):
    count = NX * NZ
    return [
        (row * count + a, row * count + b) for row in range(NY * NC) for a, b in perms[row % NC]
    ]


def around(value, axis, spread, opposite, combine):
    far = lax.ppermute(value, axis, opposite)
    near = lax.ppermute(value, axis, spread)
    return combine([value, far, near, lax.ppermute(near, "row", swap_core())])


def over_col(value, combine):
    mine = lax.axis_index("row") % NC == 0
    other = lax.ppermute(value, "row", swap_core())
    both = jnp.concatenate(
        [jnp.where(mine, value, other), jnp.where(mine, other, value)], axis=0
    )
    for shift in (shift_z, shift_x):
        both = around(both, BOTH, everywhere([shift(1), shift(-1)]), everywhere([shift(2)] * 2), combine)
    return jnp.where(mine, both[:1], both[1:])


def over_row(value, combine):
    value = combine([value, lax.ppermute(value, "row", swap_core())])
    return around(value, "row", spread_y(), shift_y(2), combine)


ORDER = (0, 1, 3, 2)


def hop_f(value, by):
    return lax.ppermute(value, BOTH, everywhere([shift_z(by), shift_x(by)]))


def hop_s(value, by):
    return lax.ppermute(value, BOTH, everywhere([shift_x(by), shift_z(by)]))


def gather(noise, latents):
    rows, width = noise.shape
    half = rows // 2
    swap = lambda v: lax.ppermute(v, "row", swap_core())
    opposite = hop_f(noise, 2)
    after, before, opposite, other = lax.optimization_barrier(
        (hop_f(noise, -1), hop_f(noise, 1), opposite, swap(latents))
    )
    line = [noise, after, before, opposite]
    near = lax.ppermute(latents, "row", spread_y())
    away = lax.ppermute(latents, "row", [(b, a) for a, b in spread_y()])
    top, end = halves_call(line)
    ready, _, _ = lax.optimization_barrier((near, top, end))
    far = lax.ppermute(ready, "row", spread_y())
    top_m, end_p = hop_s(top, 1), hop_s(end, -1)
    end_m, top_p = hop_s(end, 1), hop_s(top, -1)
    top_far, end_far = hop_s(top_m, 1), hop_s(end_p, -1)
    near_other, away_other, far_other = map(swap, lax.optimization_barrier((near, away, far)))
    split = lambda v: v.reshape(4, half, width)
    lat = [latents, other, near, near_other, away, away_other, far, far_other]
    return (
        line,
        [split(v) for v in (top_p, end_p, top_m, end_m)],
        [split(top_far), split(end_far)],
        lat,
    )


def latent_spots():
    row, col = lax.axis_index("row"), lax.axis_index("col")
    y, core = row // NC, row % NC
    block = lambda dy, flip: (y + dy) % NY * NC + (core if not flip else 1 - core)
    back = jnp.where(core == 0, 3, 1)
    rows = [
        block(0, False), block(0, True), block(back, False), block(4 - back, True),
        block(4 - back, False), block(back, True), block(2, False), block(2, True),
    ]
    at = (jnp.stack(rows)[:, None] * 2 + jnp.arange(2)[None, :]).reshape(-1)
    dx, dz = (at // NZ - col // NZ) % NX, (at % NZ - col % NZ) % NZ
    df, ds = jnp.where(core == 0, dz, dx), jnp.where(core == 0, dx, dz)
    rank = lambda d: jnp.where(d < 2, d, 5 - d)
    return (rank(ds) * 4 + rank(df)).astype(jnp.int32)


def scatter_sum(plan, spots, lat, far_top, far_end, mass, rowpot, colpot):
    barrier = lax.optimization_barrier
    far_top, far_end = hop_s(far_top, 1), hop_s(far_end, -1)
    end, top, after, before = share_call(spots, lat, plan, mass)
    end_m, top_p = hop_s(end, 1), hop_s(top, -1)
    top, end = onward_call(plan, after, before, mass, far_top, far_end)
    top_m, end_p = hop_s(top, 1), hop_s(end, -1)
    plan, rowpot, colpot, _, _ = barrier((plan, rowpot, colpot, top, end))
    own, mass = own_call(spots, lat, plan, mass, top_p, end_m)
    rowpot, colpot = rowpot * LN2, colpot * LN2
    own, top_m, end_p, rowpot, colpot = barrier((own, top_m, end_p, rowpot, colpot))
    keep, mass, *parts = sum_call(own, mass, top_m, end_p)
    parts = [hop_f(v, ORDER[k]) for v, k in zip(parts, (3, 2, 1))]
    return finish_call(keep, mass, parts), rowpot, colpot


def steps_of(total, step, body):
    def turn(i, _):
        body(pl.ds(pl.multiple_of(i * step, step), step))
        return 0

    lax.fori_loop(0, total // step, turn, 0)


def eye():
    return lax.broadcasted_iota(jnp.int32, (128, 128), 0) == lax.broadcasted_iota(
        jnp.int32, (128, 128), 1
    )


def to_lanes(column):
    mask = eye()
    return jnp.concatenate(
        [
            jnp.sum(jnp.where(mask, column[at : at + 128], 0.0), axis=0, keepdims=True)
            for at in range(0, column.shape[0], 128)
        ],
        axis=1,
    )


def to_sublanes(line):
    mask = eye()
    return jnp.concatenate(
        [
            jnp.sum(jnp.where(mask, line[:, at : at + 128], 0.0), axis=1, keepdims=True)
            for at in range(0, line.shape[1], 128)
        ],
        axis=0,
    )


TAIL = 16


def pack(mass, lanes):
    high = mass.astype(BF16).astype(F32)
    row = lax.broadcasted_iota(jnp.int32, (TAIL, lanes), 0)
    out = jnp.zeros((TAIL, lanes), F32)
    line = jnp.concatenate([high, mass - high], axis=1)
    for k in range(line.shape[1] // lanes):
        out = jnp.where(row == k, line[:, k * lanes : (k + 1) * lanes], out)
    return out.astype(BF16)


def unpack(tail, count):
    tail = tail.astype(F32)
    line = jnp.concatenate([tail[k : k + 1] for k in range(2 * count // tail.shape[1])], axis=1)
    return line[:, :count] + line[:, count:]


def row_lse_block(logits_ref, rows, colpot, lse_ref):
    step = 32
    columns = []
    for at in range(0, rows.size, step):
        t = logits_ref[pl.ds(rows.start + at, step), :] + colpot
        high = jnp.max(t, axis=1, keepdims=True)
        total = jnp.sum(jnp.exp2(t - high), axis=1, keepdims=True)
        columns.append(high + jnp.log2(total))
    lse_ref[:, rows] = to_lanes(jnp.concatenate(columns, axis=0))


WIDE = 512


def halves_kernel(*refs):
    blocks, outs, sem = refs[:4], refs[4:6], refs[6]
    half = blocks[0].shape[0] // 2
    copies = [
        pltpu.make_async_copy(
            block.at[pl.ds(part * half, half), :], out.at[pl.ds(k * half, half), :], sem.at[part, k]
        )
        for part, out in enumerate(outs)
        for k, block in enumerate(blocks)
    ]
    for copy in copies:
        copy.start()
    for copy in copies:
        copy.wait()


def halves_call(blocks):
    rows, width = blocks[0].shape
    return pl.pallas_call(
        halves_kernel,
        in_specs=[pl.BlockSpec(memory_space=pl.ANY)] * 4,
        out_specs=[pl.BlockSpec(memory_space=pl.ANY)] * 2,
        out_shape=[jax.ShapeDtypeStruct((2 * rows, width), BF16)] * 2,
        scratch_shapes=[pltpu.SemaphoreType.DMA((2, 4))],
        cost_estimate=pl.CostEstimate(
            flops=0, bytes_accessed=16 * rows * width, transcendentals=0
        ),
        compiler_params=pltpu.CompilerParams(vmem_limit_bytes=2 * 2**20),
        name="halves",
    )(*blocks)


def fetch(quarter, spot_ref, lat_refs, buf, sem):
    width = buf.shape[1] // 4
    for n in range(16):
        spot = spot_ref[n]

        @pl.when(spot // 4 == quarter)
        def start():
            lane = pl.multiple_of(lax.rem(spot, 4) * width, width)
            pltpu.make_async_copy(
                lat_refs[n // 2].at[:, pl.ds(n % 2 * width, width)], buf.at[:, pl.ds(lane, width)], sem
            ).start()


def arrive(buf, sem):
    pltpu.make_async_copy(buf, buf, sem).wait()


def near_kernel(spot_ref, *refs):
    line_refs, near_refs, lat_refs = refs[:4], refs[4:8], refs[8:16]
    cross_ref, last_ref, noise_buf, lat_buf, noise_sem, lat_sem, last_sem = refs[16:]
    half = cross_ref.shape[0] // 2
    width = line_refs[0].shape[1]

    def start(quarter):
        slot = lax.rem(quarter, 2)
        fetch(quarter, spot_ref, lat_refs, lat_buf.at[slot], lat_sem.at[slot])
        for k in range(4):
            lanes = pl.ds(k * width, width)

            @pl.when(quarter == 0)
            def whole():
                pltpu.make_async_copy(
                    line_refs[k], noise_buf.at[slot, :, lanes], noise_sem.at[slot]
                ).start()

            for part in range(4):

                @pl.when(quarter == 1 + part // 2)
                def halves():
                    pltpu.make_async_copy(
                        near_refs[part].at[k],
                        noise_buf.at[slot, pl.ds(part % 2 * half, half), lanes],
                        noise_sem.at[slot],
                    ).start()

    start(jnp.int32(0))
    fetch(3, spot_ref, lat_refs, last_ref, last_sem)

    def clear(rows):
        cross_ref[rows, :] = jnp.zeros((128, cross_ref.shape[1]), F32)

    steps_of(cross_ref.shape[0], 128, clear)

    def multiply(quarter, _):
        slot = lax.rem(quarter, 2)
        arrive(noise_buf.at[slot], noise_sem.at[slot])
        arrive(lat_buf.at[slot], lat_sem.at[slot])
        pl.when(quarter < 2)(lambda: start(quarter + 1))
        cross_ref[...] += lax.dot_general(
            noise_buf[slot], lat_buf[slot], (((1,), (1,)), ((), ())), preferred_element_type=F32
        )
        return 0

    lax.fori_loop(0, 3, multiply, 0)
    arrive(last_ref, last_sem)


def in_hbm(value):
    return pltpu.with_memory_space_constraint(value, pltpu.HBM)


def near_call(spots, line, near, lat):
    rows, width = line[0].shape
    cols = lat[0].shape[0]
    return pl.pallas_call(
        near_kernel,
        in_specs=[pl.BlockSpec(memory_space=pltpu.SMEM)] + [pl.BlockSpec(memory_space=pl.ANY)] * 16,
        out_specs=[pl.BlockSpec(memory_space=pltpu.VMEM)] * 2,
        out_shape=[
            jax.ShapeDtypeStruct((rows, cols), F32),
            jax.ShapeDtypeStruct((cols, 4 * width), BF16),
        ],
        scratch_shapes=[
            pltpu.VMEM((2, rows, 4 * width), BF16),
            pltpu.VMEM((2, cols, 4 * width), BF16),
            pltpu.SemaphoreType.DMA((2,)),
            pltpu.SemaphoreType.DMA((2,)),
            pltpu.SemaphoreType.DMA,
        ],
        cost_estimate=pl.CostEstimate(
            flops=8 * rows * cols * 12 * width,
            bytes_accessed=2 * (rows * 12 + cols * 16) * width + 4 * rows * cols,
            transcendentals=0,
        ),
        compiler_params=pltpu.CompilerParams(vmem_limit_bytes=14 * 2**20),
        name="cross_near",
    )(spots, *[in_hbm(v) for v in (*line, *near)], *[v if k % 2 else in_hbm(v) for k, v in enumerate(lat)])


def far_kernel(scale, top_ref, end_ref, lat_ref, cross_ref, logits_ref, lse_ref):
    half = top_ref.shape[1]

    for start, part_ref in ((0, top_ref), (half, end_ref)):
        rows = pl.ds(start, half)
        noise = jnp.concatenate([part_ref[k] for k in range(4)], axis=1)
        cross = lax.dot_general(
            noise, lat_ref[...], (((1,), (1,)), ((), ())), preferred_element_type=F32
        )
        logits_ref[rows, :] = (cross_ref[rows, :] + cross) * scale
        for at in range(start, start + half, 256):
            row_lse_block(logits_ref, pl.ds(at, 256), 0.0, lse_ref)


def far_call(far, lat, cross, scale):
    rows, cols = cross.shape
    out_shape = [
        jax.ShapeDtypeStruct((rows, cols), F32),
        jax.ShapeDtypeStruct((1, rows), F32),
    ]
    return in_vmem(
        functools.partial(far_kernel, scale), "cross_far", out_shape,
        2 * rows * cols * lat.shape[1], *far, lat, cross,
    )


def row_kernel(logits_ref, colpot_ref, lse_ref):
    colpot = colpot_ref[...]
    steps_of(logits_ref.shape[0], 256, lambda rows: row_lse_block(logits_ref, rows, colpot, lse_ref))


def row_call(logits, colpot):
    out_shape = [jax.ShapeDtypeStruct((1, logits.shape[0]), F32)]
    return in_vmem(row_kernel, "row_lse", out_shape, 8 * logits.size, logits, colpot)[0]


def col_kernel(logits_ref, rowpot_ref, lse_ref):
    rows, cols = logits_ref.shape
    block = 256

    def some_rows(i, parts):
        first = pl.multiple_of(i * block, block)
        rowpot = to_sublanes(rowpot_ref[:, pl.ds(first, block)])
        rowpot = jnp.broadcast_to(rowpot, (block, 128))
        lines = []
        for at in range(0, cols, 128):
            t = logits_ref[pl.ds(first, block), pl.ds(at, 128)] + rowpot
            high = jnp.max(t, axis=0, keepdims=True)
            total = jnp.sum(jnp.exp2(t - high), axis=0, keepdims=True)
            lines.append(high + jnp.log2(total))
        part = jnp.concatenate(lines, axis=1)
        row = lax.broadcasted_iota(jnp.int32, parts.shape, 0)
        return jnp.where(row == i, part, parts)

    parts = lax.fori_loop(
        0, rows // block, some_rows, jnp.full((rows // block, cols), -jnp.inf, F32)
    )
    high = jnp.max(parts, axis=0, keepdims=True)
    lse_ref[...] = high + jnp.log2(jnp.sum(jnp.exp2(parts - high), axis=0, keepdims=True))


def col_call(logits, rowpot):
    out_shape = [jax.ShapeDtypeStruct((1, logits.shape[1]), F32)]
    return in_vmem(col_kernel, "col_lse", out_shape, 8 * logits.size, logits, rowpot)[0]


def plan_kernel(logits_ref, rowpot_ref, colpot_ref, lat_ref, plan_ref, mass_ref, top_ref, end_ref):
    rows = logits_ref.shape[0]
    half = rows // 2
    colpot = colpot_ref[...]

    def make_half(block):
        sums = []
        for k in range(0, half, 64):
            at = pl.ds(block.start + k, 64)
            if k % 128 == 0:
                rowpot = to_sublanes(rowpot_ref[:, pl.ds(block.start + k, 128)])
            plan = jnp.exp2(logits_ref[at, :] + rowpot[k % 128 : k % 128 + 64] + colpot).astype(BF16)
            plan_ref[at, :] = plan
            sums.append(jnp.sum(plan.astype(F32), axis=1, keepdims=True))
        mass = to_lanes(jnp.concatenate(sums, axis=0))
        mass_ref[:, block] = mass
        share = jnp.dot(plan_ref[block, :], lat_ref[...], preferred_element_type=F32).astype(BF16)
        tail = pack(mass, lat_ref.shape[1])
        for start, out_ref in ((0, top_ref), (half, end_ref)):

            @pl.when(block.start == start)
            def put():
                out_ref[:half, :] = share
                out_ref[half:, :] = tail

    steps_of(rows, half, make_half)


def multiply_into(out_ref, plan_ref, rows, lat_ref, more_ref=None):
    here = pl.ds(0, rows.size)

    def multiply(lanes):
        share = jnp.dot(plan_ref[rows, :], lat_ref[:, lanes], preferred_element_type=F32)
        if more_ref is not None:
            share = share + more_ref[here, lanes].astype(F32)
        out_ref[here, lanes] = share.astype(out_ref.dtype)

    steps_of(lat_ref.shape[1], WIDE, multiply)


def in_vmem(kernel, name, out_shape, flops, *args):
    return pl.pallas_call(
        kernel,
        in_specs=[pl.BlockSpec(memory_space=pltpu.VMEM)] * len(args),
        out_specs=jax.tree.map(lambda _: pl.BlockSpec(memory_space=pltpu.VMEM), out_shape),
        out_shape=out_shape,
        cost_estimate=pl.CostEstimate(
            flops=flops,
            bytes_accessed=sum(a.size * a.dtype.itemsize for a in args),
            transcendentals=0,
        ),
        compiler_params=pltpu.CompilerParams(vmem_limit_bytes=24 * 2**20),
        name=name,
    )(*args)


def plan_call(logits, rowpot, colpot, lat):
    rows, cols = logits.shape
    depth = lat.shape[1]
    share = jax.ShapeDtypeStruct((rows // 2 + TAIL, depth), BF16)
    out_shape = [
        jax.ShapeDtypeStruct((rows, cols), BF16),
        jax.ShapeDtypeStruct((1, rows), F32),
        share,
        share,
    ]
    return in_vmem(
        plan_kernel, "plan", out_shape, 2 * rows * cols * depth, logits, rowpot, colpot, lat
    )


def lat_call(kernel, name, out_shape, flops, spots, lat, scratch, *args):
    space = [pltpu.SMEM] + [pl.ANY] * len(lat) + [pltpu.VMEM] * len(args)
    return pl.pallas_call(
        kernel,
        in_specs=[pl.BlockSpec(memory_space=m) for m in space],
        out_specs=[pl.BlockSpec(memory_space=pltpu.VMEM)] * len(out_shape),
        out_shape=out_shape,
        scratch_shapes=scratch,
        cost_estimate=pl.CostEstimate(
            flops=flops,
            bytes_accessed=sum(a.size * a.dtype.itemsize for a in args),
            transcendentals=0,
        ),
        compiler_params=pltpu.CompilerParams(vmem_limit_bytes=24 * 2**20),
        name=name,
    )(spots, *lat, *args)


def share_kernel(spot_ref, *refs):
    lat_refs, plan_ref, mass_ref = refs[:8], refs[8], refs[9]
    end_ref, top_ref, after_ref, before_ref, sem = refs[10:]
    half = plan_ref.shape[0] // 2
    fetch(1, spot_ref, lat_refs, after_ref, sem.at[0])
    fetch(2, spot_ref, lat_refs, before_ref, sem.at[1])
    for n, (lat_ref, out_ref, rows) in enumerate(
        ((after_ref, end_ref, pl.ds(half, half)), (before_ref, top_ref, pl.ds(0, half)))
    ):
        out_ref[half:, :] = pack(mass_ref[:, rows], out_ref.shape[1])
        arrive(lat_ref, sem.at[n])
        multiply_into(out_ref, plan_ref, rows, lat_ref)


def share_call(spots, lat, plan, mass):
    rows, cols = plan.shape
    depth = 2 * lat[0].shape[1]
    share = jax.ShapeDtypeStruct((rows // 2 + TAIL, depth), BF16)
    quarter = jax.ShapeDtypeStruct((cols, depth), BF16)
    return lat_call(
        share_kernel, "share", [share, share, quarter, quarter], 2 * rows * cols * depth,
        spots, lat, [pltpu.SemaphoreType.DMA((2,))], plan, mass,
    )


def onward_kernel(plan_ref, after_ref, before_ref, mass_ref, top_more, end_more, top_ref, end_ref):
    half = plan_ref.shape[0] // 2
    for lat_ref, more, rows, out_ref in (
        (after_ref, top_more, pl.ds(0, half), top_ref),
        (before_ref, end_more, pl.ds(half, half), end_ref),
    ):
        multiply_into(out_ref, plan_ref, rows, lat_ref, more)
        out_ref[half:, :] = pack(mass_ref[:, rows] + unpack(more[half:, :], half), out_ref.shape[1])


def onward_call(plan, after, before, mass, top_more, end_more):
    rows, cols = plan.shape
    depth = after.shape[1]
    out_shape = [jax.ShapeDtypeStruct((rows // 2 + TAIL, depth), BF16)] * 2
    return in_vmem(
        onward_kernel, "onward", out_shape, 2 * rows * cols * depth,
        plan, after, before, mass, top_more, end_more,
    )


def sum_kernel(own_ref, mass_ref, top_ref, end_ref, keep_ref, total_ref, *part_refs):
    rows = own_ref.shape[0]
    half, width = rows // 2, keep_ref.shape[1]
    for start, more in ((0, top_ref), (half, end_ref)):
        there = pl.ds(start, half)
        total_ref[:, there] = mass_ref[:, there] + unpack(more[half:, :], half)
    tail = pack(total_ref[...], width)
    for start, more in ((0, top_ref), (half, end_ref)):

        def add(here):
            there = pl.ds(start + here.start, here.size)
            for k, out_ref in zip((3, 2, 1, 0), (*part_refs, keep_ref)):
                lanes = pl.ds(k * width, width)
                value = own_ref[there, lanes] + more[here, lanes].astype(F32)
                out_ref[there, :] = value.astype(out_ref.dtype)

        steps_of(half, 128, add)
    for out_ref in part_refs:
        out_ref[rows:, :] = tail


def sum_call(own, mass, *received):
    rows, depth = own.shape
    width = depth // 4
    part = jax.ShapeDtypeStruct((rows + TAIL, width), BF16)
    out_shape = [
        jax.ShapeDtypeStruct((rows, width), F32),
        jax.ShapeDtypeStruct((1, rows), F32),
        part, part, part,
    ]
    return in_vmem(sum_kernel, "sum_s", out_shape, 2 * rows * depth, own, mass, *received)


def finish_kernel(keep_ref, total_ref, *refs):
    part_refs, out_ref = refs[:-1], refs[-1]
    rows = keep_ref.shape[0]
    mass = total_ref[...]
    for part in part_refs:
        mass = mass + unpack(part[rows:, :], rows)
    step = 128
    for at in range(0, rows, step):
        there = pl.ds(at, step)
        value = keep_ref[there, :]
        for part in part_refs:
            value = value + part[there, :].astype(F32)
        out_ref[there, :] = (value / to_sublanes(mass[:, at : at + step])).astype(BF16)


def finish_call(keep, mass, parts):
    out_shape = [jax.ShapeDtypeStruct(keep.shape, BF16)]
    return in_vmem(finish_kernel, "finish", out_shape, 4 * keep.size, keep, mass, *parts)[0]


def own_kernel(spot_ref, *refs):
    lat_refs, (plan_ref, mass_ref, top_ref, end_ref) = refs[:8], refs[8:12]
    out_ref, total_ref, lat_buf, sem = refs[12:]
    half = plan_ref.shape[0] // 2
    fetch(0, spot_ref, lat_refs, lat_buf, sem)
    arrive(lat_buf, sem)
    for rows, more in ((pl.ds(0, half), top_ref), (pl.ds(half, half), end_ref)):
        multiply_into(out_ref.at[rows, :], plan_ref, rows, lat_buf, more)
        total_ref[:, rows] = mass_ref[:, rows] + unpack(more[half:, :], half)


def own_call(spots, lat, plan, mass, top, end):
    rows, cols = plan.shape
    depth = 2 * lat[0].shape[1]
    return lat_call(
        own_kernel,
        "own",
        [jax.ShapeDtypeStruct((rows, depth), F32), jax.ShapeDtypeStruct((1, rows), F32)],
        2 * rows * cols * depth,
        spots, lat, [pltpu.VMEM((cols, depth), BF16), pltpu.SemaphoreType.DMA],
        plan, mass, top, end,
    )


def on_device(noise, latents):
    width = latents.shape[1] * lax.axis_size("row")
    noise_count = noise.shape[0] * lax.axis_size("row")
    latent_count = latents.shape[0] * lax.axis_size("col")
    line, near, far, pieces = gather(noise, latents)
    spots = latent_spots()
    cross, last = near_call(spots, line, near, pieces)
    logits, lse = far_call(far, last, cross, 2.0 / (width * EPSILON) * LOG2E)
    for step in range(ITERS):
        if step:
            lse = row_call(logits, colpot)
        rowpot = -math.log2(noise_count) - over_col(lse, logadd)
        colpot = -math.log2(latent_count) - over_row(col_call(logits, rowpot), logadd)
    plan, mass, far_top, far_end = plan_call(logits, rowpot, colpot, last)
    transported, rowpot, colpot = scatter_sum(
        plan, spots, pieces, far_top, far_end, mass, rowpot, colpot
    )
    return (transported, rowpot.reshape(-1), colpot.reshape(-1))


def solution(mesh):
    in_specs = (P("row", "col"), P("col", "row"))
    out_specs = (P("row", "col"), P("row"), P("col"))
    return jax.shard_map(
        on_device, mesh=mesh, in_specs=in_specs, out_specs=out_specs, check_vma=False
    )
```
